256 devices in a mesh: dp: 64 (over z, x, core), mp: 4 (over y).
Axes of the slice: x: 4, y: 4, z: 8, core: 2. Of those that a mesh axis runs over, the one named last changes fastest.
Arguments:
- query_text_memory: bfloat16 [2, 64, 64, 4096], P(None, 'dp', None, 'mp'), may hold values from -1.5 to 1.5
- query_text_feed: bfloat16 [64, 64, 4096], P('dp', None, 'mp'), may hold values from -6 to 6
- reply_acceptor_memory: bfloat16 [3, 128, 64, 4096], P(None, 'dp', None, 'mp'), may hold values from -1.5 to 1.5
- reply_feed: bfloat16 [128, 64, 4096], P('dp', None, 'mp'), may hold values from -6 to 6
- reply_cotangent_vector: bfloat16 [128, 64, 4096], P('dp', None, 'mp'), may hold values from -6 to 6
- query_placement: int32 [64], replicated, may hold values from 0 to 63, each once
- reply_parent_query: int32 [128], replicated, may hold values from 0 to 63, as said below
- fading_narrowing: float32 [4096, 128], P('mp'), may hold values from -0.09375 to 0.09375
- fading_widening: float32 [128, 4096], P(None, 'mp'), may hold values from -0.5 to 0.5
- fading_anchor_rate: float32 [4096], P('mp'), may hold values from -8 to -2
- self_emphasis: float32 [4096], P('mp'), may hold values from 0.2 to 1.5
- lagged_token_fraction: float32 [4096], P('mp'), may hold values from 0.05 to 0.95
Outputs:
- response_rkv_grad: bfloat16 [3, 128, 64, 4096], P(None, 'dp', None, 'mp')
- response_x_grad: bfloat16 [128, 64, 4096], P('dp', None, 'mp')
- prompt_kv_grad: bfloat16 [2, 64, 64, 4096], P(None, 'dp', None, 'mp')
- prompt_x_grad: bfloat16 [64, 64, 4096], P('dp', None, 'mp')
- lora_down_grad: float32 [4096, 128], P('mp')
- lora_up_grad: float32 [128, 4096], P(None, 'mp')
- decay_base_grad: float32 [4096], P('mp')
- self_emphasis_adjoint: float32 [4096], P('mp')
- shift_mix_grad: float32 [4096], P('mp')
The draws below stay inside these ranges and needn't reach their ends.
Inputs may be any that keep to these rules, and one draw needn't show every extreme that they name: `reply_parent_query`: each prompt is named by exactly 2 responses.
All inputs are finite; a program needn't handle non-finite values.
Results may differ from the reference program's by a relative error of at most 0.0015.
Values sent between devices are 32-bit elements; how exact they have to be, the bound alone decides.
A program may use at most 128 MiB of HBM per device.

```python
import jax
import jax.numpy as jnp
from jax import lax

EMBED_SIZE = 4096
DECAY_RANK = 128
CHANNEL_COUNT = 64
BLK = 16
L_PROMPT = 64
L_RESP = 64
PROMPTS = 64
RESPONSES = 128
GROUP = 2


def draw_reply_parent_query(key, part):
    key = jax.random.fold_in(key, 11)
    return (jax.random.permutation(key, RESPONSES) // GROUP).astype(jnp.int32)


def draw_fading_anchor_rate(key, part):
    key = jax.random.fold_in(key, 23)
    return jax.random.uniform(key, (EMBED_SIZE,), jnp.float32, -7.0, -2.0)


def block_scale(stream_key, dims, split, low, high):
    loudness = 1.0
    for position, blocks in split:
        steps = jax.random.uniform(jax.random.fold_in(jax.random.fold_in(stream_key, 6), position), (blocks,), jnp.float32, low / len(split), high / len(split))
        loudness = loudness * jnp.repeat(jnp.exp(steps), dims[position] // blocks).reshape((-1,) + (1,) * (len(dims) - 1 - position))
    return loudness


def scatter_about(key, extent, deviation, most, cuts=(), kind=jnp.bfloat16):
    level = block_scale(key, extent, cuts, -0.22, 0.18) if cuts else 1.0
    entries = jax.random.normal(key, extent, jnp.float32) * deviation * level
    return jnp.minimum(jnp.maximum(entries, -most), most).astype(kind)


def setup_inputs(seed: int = 0) -> dict:
    arg_keys = jax.random.split(jax.random.key(seed), 13)
    query_text_memory = scatter_about(arg_keys[0], (2, PROMPTS, L_PROMPT, EMBED_SIZE), 0.25, 1.5, ((1, 64), (3, 4)))
    query_text_feed = scatter_about(arg_keys[1], (PROMPTS, L_PROMPT, EMBED_SIZE), 1.0, 6.0, ((0, 64), (2, 4)))
    reply_acceptor_memory = scatter_about(arg_keys[2], (3, RESPONSES, L_RESP, EMBED_SIZE), 0.25, 1.5, ((1, 64), (3, 4)))
    reply_feed = scatter_about(arg_keys[3], (RESPONSES, L_RESP, EMBED_SIZE), 1.0, 6.0, ((0, 64), (2, 4)))
    reply_cotangent_vector = scatter_about(arg_keys[4], (RESPONSES, L_RESP, EMBED_SIZE), 1.0, 6.0, ((0, 64), (2, 4)))
    query_placement = jax.random.permutation(arg_keys[5], PROMPTS).astype(jnp.int32)
    reply_parent_query = draw_reply_parent_query(jax.random.fold_in(arg_keys[12], 71), 0)
    fading_narrowing = scatter_about(arg_keys[7], (EMBED_SIZE, DECAY_RANK), EMBED_SIZE ** -0.5, 0.09375, ((0, 4),), jnp.float32)
    fading_widening = scatter_about(arg_keys[8], (DECAY_RANK, EMBED_SIZE), DECAY_RANK ** -0.5, 0.5, ((1, 4),), jnp.float32)
    fading_anchor_rate = draw_fading_anchor_rate(jax.random.fold_in(arg_keys[12], 71), 0)
    self_emphasis = jnp.clip(0.2 + 1.3 * jax.random.uniform(arg_keys[10], (EMBED_SIZE,), jnp.float32) ** block_scale(arg_keys[10], (EMBED_SIZE,), ((0, 4),), -0.2, 0.2), 0.2, 1.5)
    lagged_token_fraction = jnp.clip(0.05 + 0.9 * jax.random.uniform(arg_keys[11], (EMBED_SIZE,), jnp.float32) ** block_scale(arg_keys[11], (EMBED_SIZE,), ((0, 4),), -0.2, 0.2), 0.05, 0.95)
    return {"query_text_memory": query_text_memory, "query_text_feed": query_text_feed, "reply_acceptor_memory": reply_acceptor_memory, "reply_feed": reply_feed, "reply_cotangent_vector": reply_cotangent_vector, "query_placement": query_placement, "reply_parent_query": reply_parent_query, "fading_narrowing": fading_narrowing, "fading_widening": fading_widening, "fading_anchor_rate": fading_anchor_rate, "self_emphasis": self_emphasis, "lagged_token_fraction": lagged_token_fraction}


highest_precision = lax.Precision.HIGHEST

def mixing_input(input_rows, leading_row, lagged_token_fraction, fading_narrowing):
    previous = jnp.concatenate([leading_row[None, :], input_rows[:-1]], axis=0)
    mixed_input = input_rows + (previous - input_rows) * lagged_token_fraction
    return jnp.dot(mixed_input, fading_narrowing, precision=highest_precision, preferred_element_type=jnp.float32)

def decay_row_values(hidden_entries, fading_widening, fading_anchor_rate):
    return -jnp.exp(fading_anchor_rate + jnp.dot(jnp.tanh(hidden_entries), fading_widening, precision=highest_precision, preferred_element_type=jnp.float32))

def segment_summands(memory_amount, element_sequence, self_emphasis_grouped):
    acceptor_entries, address_entries, values, log_rows = element_sequence
    cumulative = jnp.cumsum(log_rows, axis=0)
    before = cumulative - log_rows
    count = address_entries.shape[0]
    earlier = (jnp.arange(count)[:, None] > jnp.arange(count)[None, :])[:, :, None, None]
    log_gap = jnp.where(earlier, before[:, None] - cumulative[None, :], 0.0)
    decay = jnp.where(earlier, jnp.exp(log_gap), 0.0)
    scores = jnp.einsum('thc,shc,tshc->hts', acceptor_entries, address_entries, decay, precision=highest_precision)
    self_token_addend = lax.optimization_barrier(jnp.sum(acceptor_entries * self_emphasis_grouped * address_entries, axis=2))
    output_rows = jnp.einsum('hts,shd->thd', scores, values, precision=highest_precision) + self_token_addend[:, :, None] * values
    output_rows = output_rows + jnp.einsum('thc,hcd->thd', acceptor_entries * jnp.exp(before), memory_amount, precision=highest_precision)
    block_end = cumulative[-1]
    memory_amount = jnp.exp(block_end)[:, :, None] * memory_amount + jnp.einsum('shc,shd->hcd', address_entries * jnp.exp(block_end[None] - cumulative), values, precision=highest_precision)
    return (memory_amount, output_rows)

def reply_entries_group(hidden_entries, opening_amount, threefold_bundle, fading_widening, fading_anchor_rate, self_emphasis):
    log_values = decay_row_values(hidden_entries, fading_widening, fading_anchor_rate)
    length, channels = log_values.shape
    channel_groups = channels // CHANNEL_COUNT
    shape = (length // BLK, BLK, channel_groups, CHANNEL_COUNT)
    self_emphasis_grouped = self_emphasis.reshape(channel_groups, CHANNEL_COUNT)

    def advance(memory_amount, element_sequence):
        return segment_summands(memory_amount, element_sequence, self_emphasis_grouped)
    ending, output_rows = lax.scan(jax.checkpoint(advance), opening_amount, (threefold_bundle[0].reshape(shape), threefold_bundle[1].reshape(shape), threefold_bundle[2].reshape(shape), log_values.reshape(shape)))
    return output_rows.reshape(length, channels)

def prompt_recurrence_core(hidden_entries, pair_tuple, fading_widening, fading_anchor_rate):
    log_values = decay_row_values(hidden_entries, fading_widening, fading_anchor_rate)
    length, channels = log_values.shape
    channel_groups = channels // CHANNEL_COUNT
    shape = (length // BLK, BLK, channel_groups, CHANNEL_COUNT)

    def advance(memory_amount, element_sequence):
        address_entries, values, log_rows = element_sequence
        cumulative = jnp.cumsum(log_rows, axis=0)
        block_end = cumulative[-1]
        carried = jnp.exp(block_end)[:, :, None] * memory_amount
        return (carried + jnp.einsum('shc,shd->hcd', address_entries * jnp.exp(block_end[None] - cumulative), values, precision=highest_precision), None)
    opening_amount = jnp.zeros((channel_groups, CHANNEL_COUNT, CHANNEL_COUNT), jnp.float32)
    memory_amount, unused = lax.scan(jax.checkpoint(advance), opening_amount, (pair_tuple[0].reshape(shape), pair_tuple[1].reshape(shape), log_values.reshape(shape)))
    return memory_amount

def reference(query_text_memory, query_text_feed, reply_acceptor_memory, reply_feed, reply_cotangent_vector, query_placement, reply_parent_query, fading_narrowing, fading_widening, fading_anchor_rate, self_emphasis, lagged_token_fraction):
    matches = (query_placement[None, :] == reply_parent_query[:, None]).astype(jnp.int32)
    owner = lax.optimization_barrier(jnp.sum(jnp.arange(PROMPTS, dtype=jnp.int32)[None, :] * matches, axis=1)).astype(jnp.int32)

    def onward_sweep(couple_segment, query_segment, threefold_segment, reply_segment, narrowing_grid, widening_grid, fading_anchor_coeffs, self_emphasis_grid, blend_coeffs):
        blank_row = jnp.zeros((EMBED_SIZE,), jnp.float32)

        def one_prompt(item):
            pair_tuple, rows = item
            hidden_entries = mixing_input(rows, blank_row, blend_coeffs, narrowing_grid)
            return prompt_recurrence_core(hidden_entries, pair_tuple, widening_grid, fading_anchor_coeffs)
        states = lax.map(jax.checkpoint(one_prompt), (jnp.moveaxis(couple_segment, 1, 0), query_segment))
        start_values = states[owner]
        firsts = query_segment[:, -1][owner]

        def one_response(item):
            opening_amount, first, threefold_bundle, rows = item
            hidden_entries = mixing_input(rows, first, blend_coeffs, narrowing_grid)
            return reply_entries_group(hidden_entries, opening_amount, threefold_bundle, widening_grid, fading_anchor_coeffs, self_emphasis_grid)
        return lax.map(jax.checkpoint(one_response), (start_values, firsts, jnp.moveaxis(threefold_segment, 1, 0), reply_segment))
    emitted_results, reverse_sweep = jax.vjp(onward_sweep, query_text_memory.astype(jnp.float32), query_text_feed.astype(jnp.float32), reply_acceptor_memory.astype(jnp.float32), reply_feed.astype(jnp.float32), fading_narrowing, fading_widening, fading_anchor_rate, self_emphasis, lagged_token_fraction)
    grads = reverse_sweep(reply_cotangent_vector.astype(jnp.float32))
    return (grads[2].astype(jnp.bfloat16), grads[3].astype(jnp.bfloat16), grads[0].astype(jnp.bfloat16), grads[1].astype(jnp.bfloat16), grads[4], grads[5], grads[6], grads[7], grads[8])
```

```python
import functools

import jax
import jax.numpy as jnp
import numpy as np
from jax import lax
from jax.experimental import pallas as pl
from jax.experimental.pallas import tpu as pltpu
from jax.sharding import PartitionSpec as P

HEAD = 64
T = 64
LANES = 128
RANK = 128
LEVELS = (32, 16, 8, 4, 2, 1)
MESH = pl.DeviceIdType.MESH
F32 = jnp.float32
BF16 = jnp.bfloat16


def stages_of(devices):
    if devices == 64:
        return ((1, 2), (2, 4), (8, 8))
    return ((1, 2), (2, 2), (4, devices // 4))


def gap_masks():
    t = np.arange(T)[:, None]
    j = np.arange(T)[None, :]
    rows = []
    for b in LEVELS:
        same = (t // (2 * b)) == (j // (2 * b))
        mid = (t // (2 * b)) * 2 * b + b
        second = (t % (2 * b)) >= b
        rows.append(same & np.where(second, (j >= mid) & (j < t), (j > t) & (j < mid)))
    rows.append(j < t)
    return np.concatenate(rows, axis=0).astype(np.float32)


def level_masks():
    t = np.arange(T)[:, None]
    s = (np.arange(2 * T) % T)[None, :]
    rows = []
    for b in LEVELS:
        same = (t // (2 * b)) == (s // (2 * b))
        rows.append(same & ((t % (2 * b) >= b) != (s % (2 * b) >= b)))
    return np.concatenate(rows, axis=0).astype(np.float32)


def nn(a, b):
    return lax.dot_general(a, b, (((1,), (0,)), ((), ())), preferred_element_type=F32)


def nt(a, b):
    return lax.dot_general(a, b, (((1,), (1,)), ((), ())), preferred_element_type=F32)


def tn(a, b):
    return lax.dot_general(a, b, (((0,), (0,)), ((), ())), preferred_element_type=F32)


def split(x):
    hi = x.astype(BF16)
    return hi, (x - hi.astype(F32)).astype(BF16)


def split3(x):
    hi = x.astype(BF16)
    rest = x - hi.astype(F32)
    mid = rest.astype(BF16)
    return hi, mid, (rest - mid.astype(F32)).astype(BF16)


def dot3(dot, a, b):
    return dot(a[0], b[0]) + (dot(a[0], b[1]) + dot(a[1], b[0]))


def left2(dot, a, b):
    return dot(a[0], b) + dot(a[1], b)


def right2(dot, a, b):
    return dot(a, b[0]) + dot(a, b[1])


def lane_head(shape):
    return lax.broadcasted_iota(jnp.int32, shape, len(shape) - 1) < HEAD


def block_diag(x):
    low = lane_head(x.shape)
    zero = jnp.zeros_like(x)
    return jnp.concatenate([jnp.where(low, x, zero), jnp.where(low, zero, x)], axis=0)


def pack_diag(m):
    return jnp.where(lane_head((HEAD, LANES)), m[:HEAD], m[HEAD:])


def body(
    devices,
    ranks,
    channels,
    owner_ref,
    child_ref,
    kv_ref,
    xp_ref,
    rkv_ref,
    xr_ref,
    dy_ref,
    down_ref,
    up_ref,
    base_ref,
    u_ref,
    f_ref,
    gaps_ref,
    gaps_t_ref,
    masks_ref,
    rkv_out,
    xr_out,
    kv_out,
    xp_out,
    down_out,
    up_out,
    vec_out,
    row_src,
    row_land,
    mixed,
    hid,
    hid_land,
    lead,
    lead_land,
    dec,
    ef,
    send1,
    recv1,
    send2,
    recv2,
    dr_loc,
    dd_loc,
    th_ref,
    dz_ref,
    dth,
    dth_land,
    dh_src,
    dh_land,
    vec,
    vec_land,
    grad,
    cur1,
    cur2,
    cur3,
    land0,
    land1,
    land2,
    fin,
    row_s,
    row_r,
    hid_s,
    hid_r,
    lead_s,
    lead_r,
    r1_s,
    r1_r,
    r2_s,
    r2_r,
    dth_s,
    dth_r,
    dh_s,
    dh_r,
    vec_s,
    vec_r,
    rs_s,
    rs_r,
    ag_s,
    ag_r,
):
    me = lax.axis_index("dp")
    rank = lax.axis_index("mp")
    pairs = channels // LANES
    per = HEAD * pairs // devices
    dests = HEAD // per
    stages = stages_of(devices)

    def lanes(p):
        return pl.ds(pl.multiple_of(p * LANES, LANES), LANES)

    def rows_of(p):
        return pl.ds(pl.multiple_of(p * LANES, LANES), LANES)

    def loop(n, fn, init=None):
        if init is None:
            lax.fori_loop(0, n, lambda i, c: (fn(i), c)[1], 0)
            return None
        return lax.fori_loop(0, n, fn, init)

    def remote(src, dst, ssem, rsem, axis, peer):
        return pltpu.make_async_remote_copy(
            src_ref=src,
            dst_ref=dst,
            send_sem=ssem,
            recv_sem=rsem,
            device_id={axis: peer},
            device_id_type=MESH,
        )

    def bulk_wait(view, sem):
        pltpu.make_async_copy(view, view, sem).wait()

    barrier = pltpu.get_barrier_semaphore()

    def greet(i):
        pl.semaphore_signal(
            barrier, inc=1, device_id={"dp": lax.rem(me + 1 + i, devices)}, device_id_type=MESH
        )

    loop(devices - 1, greet)
    for i in range(1, ranks):
        pl.semaphore_signal(
            barrier, inc=1, device_id={"mp": lax.rem(rank + i, ranks)}, device_id_type=MESH
        )

    row_src[...] = xp_ref[0, T - 16 :, :].astype(F32)[15:16]
    pl.semaphore_wait(barrier, devices - 1 + ranks - 1)

    def send_row(i):
        peer = lax.rem(me + 1 + i, devices)
        remote(row_src, row_land.at[me], row_s, row_r, "dp", peer).start()

    loop(devices - 1, send_row)
    row_land[me] = row_src[...]

    first_row = lax.broadcasted_iota(jnp.int32, (T, LANES), 0) == 0
    last_row = lax.broadcasted_iota(jnp.int32, (T, LANES), 0) == T - 1

    def x_of(i, p):
        return (xp_ref[0, :, lanes(p)] if i == 0 else xr_ref[i - 1, :, lanes(p)]).astype(F32)

    def mix(p, acc):
        f = f_ref[:, lanes(p)]
        parts = []
        for i in range(3):
            x = x_of(i, p)
            prev = jnp.where(first_row, 0.0, pltpu.roll(x, 1, 0))
            m = x + (prev - x) * f
            mixed[i * T : (i + 1) * T, lanes(p)] = m
            parts.append(m)
        return acc + dot3(nn, split(jnp.concatenate(parts, axis=0)), split(down_ref[rows_of(p), :]))

    hid[...] = loop(pairs, mix, jnp.zeros((3 * T, RANK), F32))

    def exchange(src, land, ssem, rsem):
        for i in range(1, ranks):
            peer = lax.rem(rank + i, ranks)
            remote(src, land.at[rank], ssem.at[i], rsem.at[rank], "mp", peer).start()
        land[rank] = src[...]

    def exchanged(land, rsem):
        for i in range(1, ranks):
            source = lax.rem(rank + i, ranks)
            bulk_wait(land.at[source], rsem.at[source])
        total = land[0]
        for i in range(1, ranks):
            total = total + land[i]
        return total

    exchange(hid, hid_land, hid_s, hid_r)

    bulk_wait(row_land.at[pl.ds(0, devices - 1)], row_r)
    owners = [owner_ref[2 * me + i] for i in range(2)]
    lead_rows = [row_land[o] for o in owners]
    row8 = lax.broadcasted_iota(jnp.int32, (8, channels), 0)
    both = jnp.where(row8 == 0, lead_rows[0], jnp.where(row8 == 1, lead_rows[1], 0.0))
    lead[:, :] = both

    def lead_mix(p, acc):
        fl = f_ref[:, lanes(p)] * lead[:, lanes(p)]
        for i in range(2):
            at = (i + 1) * T
            mixed[at : at + 1, lanes(p)] = mixed[at : at + 1, lanes(p)] + fl[i : i + 1]
        return acc + dot3(nn, split(fl), split(down_ref[rows_of(p), :]))

    lead_hid = loop(pairs, lead_mix, jnp.zeros((8, RANK), F32))
    dh_src[...] = lead_hid
    exchange(dh_src, lead_land, lead_s, lead_r)
    hidden = exchanged(hid_land, hid_r)
    extra = exchanged(lead_land, lead_r)
    th_ref[...] = jnp.tanh(hidden)
    for i in range(2):
        at = (i + 1) * T
        th_ref[at : at + 1, :] = jnp.tanh(hidden[at : at + 1] + extra[i : i + 1])

    before = gaps_ref[len(LEVELS) * T :, :]
    suffix = (
        lax.broadcasted_iota(jnp.int32, (T, T), 1) > lax.broadcasted_iota(jnp.int32, (T, T), 0)
    ).astype(BF16)

    def exact(mask, x):
        hi, mid, low = split3(x)
        return nn(mask, hi) + (nn(mask, mid) + nn(mask, low))

    def decays(p):
        th = split(th_ref[...])
        z = dot3(nn, th, split(up_ref[:, lanes(p)])) + base_ref[:, lanes(p)]
        d = -jnp.exp(z)
        dec[:, lanes(p)] = d
        for i in range(3):
            e = jnp.exp(exact(suffix if i == 0 else before, d[i * T : (i + 1) * T]))
            ef[i * T : (i + 1) * T, lanes(p)] = e
            if i == 0:
                a, b = kv_ref[0, 0, :, lanes(p)], kv_ref[1, 0, :, lanes(p)]
            else:
                a, b = rkv_ref[0, i - 1, :, lanes(p)], dy_ref[i - 1, :, lanes(p)]
            packed = pack_diag(left2(tn, split(a.astype(F32) * e), b))
            send1[pl.ds(p * dests, dests), i] = packed.reshape(dests, per, LANES)

    loop(pairs, decays)

    def route1(i):
        peer = lax.rem(me + 1 + i, devices)
        remote(send1.at[peer], recv1.at[pl.ds(3 * me, 3)], r1_s, r1_r, "dp", peer).start()

    loop(devices - 1, route1)
    recv1[pl.ds(3 * me, 3)] = send1[me]

    ones_block = (
        (lax.broadcasted_iota(jnp.int32, (LANES, LANES), 0) < HEAD)
        == (lax.broadcasted_iota(jnp.int32, (LANES, LANES), 1) < HEAD)
    ).astype(BF16)
    t_row = lax.broadcasted_iota(jnp.int32, (T, LANES), 0)
    s_col = lax.rem(lax.broadcasted_iota(jnp.int32, (T, LANES), 1), T)

    def inner(i, p):
        rb, kb, vb = (rkv_ref[n, i, :, lanes(p)] for n in range(3))
        yb = dy_ref[i, :, lanes(p)]
        r, k, v, y = (a.astype(F32) for a in (rb, kb, vb, yb))
        d = dec[pl.ds((i + 1) * T, T), lanes(p)]
        u = u_ref[:, lanes(p)]
        y_diag = block_diag(yb)
        sym = jnp.where(t_row > s_col, nt(yb, block_diag(vb)), nt(vb, y_diag))
        gap = exact(gaps_ref[: len(LEVELS) * T, :], d)
        att = jnp.zeros((T, LANES), F32)
        dr = jnp.zeros((T, LANES), F32)
        dk = jnp.zeros((T, LANES), F32)
        dgaps = []
        for level, b in enumerate(LEVELS):
            second = lax.rem(t_row, 2 * b) >= b
            mask = masks_ref[level * T : (level + 1) * T, :]
            x = jnp.exp(gap[level * T : (level + 1) * T])
            w = jnp.where(second, r, k) * x
            ws = split(w)
            wd = tuple(block_diag(a) for a in ws)
            att = att + mask * dot3(nt, ws, wd)
            dw = dot3(nn, split(mask * sym), wd)
            dgaps.append(w * dw)
            g = x * dw
            dr = dr + jnp.where(second, g, 0.0)
            dk = dk + jnp.where(second, 0.0, g)
        dgap = jnp.concatenate(dgaps, axis=0)
        dd_loc[i, :, lanes(p)] = right2(nn, gaps_t_ref[:, : len(LEVELS) * T], split(dgap))
        self_a = left2(nn, split(r * u * k), ones_block)
        self_b = left2(nn, split(y * v), ones_block)
        dv = left2(nn, split(jnp.where(s_col > t_row, att, 0.0)), y_diag) + self_a * y
        dr_loc[i, :, lanes(p)] = dr + u * k * self_b
        rkv_out[1, i, :, lanes(p)] = (dk + u * r * self_b).astype(BF16)
        rkv_out[2, i, :, lanes(p)] = dv.astype(BF16)
        part = jnp.sum(r * k * self_b, axis=0, keepdims=True)
        if i == 0:
            vec[1, :, lanes(p)] = part
        else:
            vec[1, :, lanes(p)] = vec[1, :, lanes(p)] + part

    loop(pairs, functools.partial(inner, 0))

    bulk_wait(recv1.at[pl.ds(0, 3 * (devices - 1))], r1_r)

    def shuffle(n):
        send2[n, 0] = recv1[owner_ref[2 * n] * 3]
        send2[n, 1] = recv1[owner_ref[2 * n + 1] * 3]
        send2[n, 2] = recv1[child_ref[2 * n]] + recv1[child_ref[2 * n + 1]]

    loop(devices, shuffle)

    def route2(i):
        peer = lax.rem(me + 1 + i, devices)
        remote(send2.at[peer], recv2.at[me], r2_s, r2_r, "dp", peer).start()

    loop(devices - 1, route2)
    recv2[me] = send2[me]
    loop(pairs, functools.partial(inner, 1))
    bulk_wait(recv2.at[pl.ds(0, devices - 1)], r2_r)

    def outer(p):
        for i in range(3):
            state = recv2[pl.ds(p * dests, dests), (i + 2) % 3].reshape(HEAD, LANES)
            sd = tuple(block_diag(a) for a in split(state))
            e = ef[i * T : (i + 1) * T, lanes(p)]
            if i == 0:
                kb, vb = kv_ref[0, 0, :, lanes(p)], kv_ref[1, 0, :, lanes(p)]
                k = kb.astype(F32)
                dk = e * right2(nt, vb, sd)
                dv = dot3(nn, split(k * e), sd)
                kv_out[0, 0, :, lanes(p)] = dk.astype(BF16)
                kv_out[1, 0, :, lanes(p)] = dv.astype(BF16)
                dd = right2(nn, before, split(k * dk))
            else:
                r = rkv_ref[0, i - 1, :, lanes(p)].astype(F32)
                drs = e * right2(nt, dy_ref[i - 1, :, lanes(p)], sd)
                rkv_out[0, i - 1, :, lanes(p)] = (dr_loc[i - 1, :, lanes(p)] + drs).astype(BF16)
                dd = right2(nn, suffix, split(r * drs)) + dd_loc[i - 1, :, lanes(p)]
            dz_ref[i * T : (i + 1) * T, lanes(p)] = dd * dec[i * T : (i + 1) * T, lanes(p)]

    loop(pairs, outer)

    def dth_part(p, acc):
        return acc + dot3(nt, split(dz_ref[:, lanes(p)]), split(up_ref[:, lanes(p)]))

    dth[...] = loop(pairs, dth_part, jnp.zeros((3 * T, RANK), F32))
    exchange(dth, dth_land, dth_s, dth_r)

    place = [lax.rem(me // g, n) for g, n in stages]
    size = [channels]
    for g, n in stages:
        size.append(size[-1] // n)
    lands = (land0, land1, land2)
    sums = (cur1, cur2, cur3)

    def rs_start(half, stage):
        g, n = stages[stage]
        q, rows = place[stage], size[stage + 1]
        src = grad.at[half] if stage == 0 else sums[stage - 1].at[half]
        for i in range(1, n):
            other = lax.rem(q + i, n)
            remote(
                src.at[pl.ds(pl.multiple_of(other * rows, 8), rows)],
                lands[stage].at[half, q],
                rs_s.at[half, stage, i],
                rs_r.at[half, stage, q],
                "dp",
                me + (other - q) * g,
            ).start()

    def rs_finish(half, stage):
        g, n = stages[stage]
        q, rows = place[stage], size[stage + 1]
        src = grad.at[half] if stage == 0 else sums[stage - 1].at[half]
        total = src[pl.ds(pl.multiple_of(q * rows, 8), rows), :]
        for i in range(1, n):
            other = lax.rem(q + i, n)
            bulk_wait(lands[stage].at[half, other], rs_r.at[half, stage, other])
            total = total + lands[stage][half, other]
        sums[stage][half] = total

    offs = [0]
    for stage in range(3):
        offs.append(offs[-1] + place[stage] * size[stage + 1])

    def piece(half, stage, q):
        rows = size[stage + 1]
        return fin.at[half, pl.ds(pl.multiple_of(offs[stage] + q * rows, 8), rows)]

    def ag_start(half, stage):
        g, n = stages[stage]
        q = place[stage]
        if stage == 2:
            fin[half, pl.ds(pl.multiple_of(offs[3], 8), size[3]), :] = sums[2][half]
        for i in range(1, n):
            other = lax.rem(q + i, n)
            mine = piece(half, stage, q)
            remote(
                mine,
                mine,
                ag_s.at[half, stage, i],
                ag_r.at[half, stage, q],
                "dp",
                me + (other - q) * g,
            ).start()

    def ag_finish(half, stage):
        g, n = stages[stage]
        q = place[stage]
        for i in range(1, n):
            other = lax.rem(q + i, n)
            bulk_wait(piece(half, stage, other), ag_r.at[half, stage, other])

    def vec_start(stage):
        g, n = stages[stage]
        q = place[stage]
        at = sum(m for _, m in stages[:stage])
        for i in range(1, n):
            other = lax.rem(q + i, n)
            remote(
                vec.at[pl.ds(3 * stage, 3)],
                vec_land.at[at + q],
                vec_s.at[stage, i],
                vec_r.at[stage, q],
                "dp",
                me + (other - q) * g,
            ).start()
        vec_land[at + q] = vec[3 * stage : 3 * stage + 3]

    def vec_finish(stage):
        g, n = stages[stage]
        q = place[stage]
        at = sum(m for _, m in stages[:stage])
        for i in range(1, n):
            other = lax.rem(q + i, n)
            bulk_wait(vec_land.at[at + other], vec_r.at[stage, other])
        total = vec_land[at]
        for i in range(1, n):
            total = total + vec_land[at + i]
        if stage == 2:
            vec_out[...] = total
        else:
            vec[3 * stage + 3 : 3 * stage + 6] = total

    def up_grads(p):
        dz = dz_ref[:, lanes(p)]
        grad[0, rows_of(p), :] = dot3(tn, split(th_ref[...]), split(dz))
        vec[0, :, lanes(p)] = jnp.sum(dz, axis=0, keepdims=True)

    loop(pairs, up_grads)
    rs_start(0, 0)

    th = th_ref[...]
    dh = exchanged(dth_land, dth_r) * (1.0 - th * th)
    row8h = lax.broadcasted_iota(jnp.int32, (8, RANK), 0)
    for i in range(1, ranks):
        bulk_wait(lead_land.at[0], lead_s.at[i])
        bulk_wait(dth_land.at[0], dth_s.at[i])
    dth[...] = dh
    dh_src[...] = jnp.where(
        row8h == 0, dh[T : T + 1], jnp.where(row8h == 1, dh[2 * T : 2 * T + 1], 0.0)
    )

    def send_dh(i):
        peer = lax.rem(me + 1 + i, devices)
        remote(dh_src, dh_land.at[me], dh_s, dh_r, "dp", peer).start()

    loop(devices - 1, send_dh)
    dh_land[me] = dh_src[...]

    def down_grads(p):
        grad[1, rows_of(p), :] = dot3(tn, split(mixed[:, lanes(p)]), split(dth[...]))

    loop(pairs, down_grads)
    rs_start(1, 0)

    bulk_wait(dh_land.at[pl.ds(0, devices - 1)], dh_r)
    from_children = jnp.zeros((8, RANK), F32)
    for i in range(2):
        c = child_ref[2 * me + i]
        slot = lax.div(c, 3)
        which = lax.rem(c, 3)
        rows = dh_land[slot]
        from_children = from_children + jnp.sum(
            jnp.where(row8h == which - 1, rows, 0.0), axis=0, keepdims=True
        )

    def x_grads(p):
        f = f_ref[:, lanes(p)]
        n = split(down_ref[rows_of(p), :])
        dm = dot3(nt, split(dth[...]), n)
        late = dot3(nt, split(from_children), n)[0:1]
        mix_sum = jnp.zeros((1, LANES), F32)
        for i in range(3):
            x = x_of(i, p)
            g = dm[i * T : (i + 1) * T]
            ahead = pltpu.roll(g, T - 1, 0)
            if i == 0:
                first = jnp.zeros((1, LANES), F32)
                ahead = jnp.where(last_row, late, ahead)
            else:
                first = lead[i - 1 : i, lanes(p)]
                ahead = jnp.where(last_row, 0.0, ahead)
            prev = jnp.where(first_row, first, pltpu.roll(x, 1, 0))
            dx = g + (ahead - g) * f
            mix_sum = mix_sum + jnp.sum(g * (prev - x), axis=0, keepdims=True)
            if i == 0:
                xp_out[0, :, lanes(p)] = dx.astype(BF16)
            else:
                xr_out[i - 1, :, lanes(p)] = dx.astype(BF16)
        vec[2, :, lanes(p)] = mix_sum

    rs_finish(0, 0)
    rs_start(0, 1)
    loop(pairs, x_grads)
    vec_start(0)
    rs_finish(1, 0)
    rs_start(1, 1)
    rs_finish(0, 1)
    rs_start(0, 2)
    vec_finish(0)
    vec_start(1)
    rs_finish(1, 1)
    rs_start(1, 2)
    rs_finish(0, 2)
    ag_start(0, 2)
    vec_finish(1)
    vec_start(2)
    rs_finish(1, 2)
    ag_start(1, 2)
    ag_finish(0, 2)
    ag_start(0, 1)
    vec_finish(2)
    ag_finish(1, 2)
    ag_start(1, 1)
    ag_finish(0, 1)
    ag_start(0, 0)
    ag_finish(1, 1)
    ag_start(1, 0)
    ag_finish(0, 0)

    def put_up(p):
        up_out[:, lanes(p)] = fin[0, rows_of(p), :]

    loop(pairs, put_up)
    ag_finish(1, 0)
    down_out[...] = fin[1]

    bulk_wait(row_land.at[pl.ds(0, devices - 1)], row_s)
    bulk_wait(recv1.at[pl.ds(0, 3 * (devices - 1))], r1_s)
    bulk_wait(recv2.at[pl.ds(0, devices - 1)], r2_s)
    bulk_wait(dh_land.at[pl.ds(0, devices - 1)], dh_s)
    for i in range(1, ranks):
        bulk_wait(hid_land.at[0], hid_s.at[i])
    for stage, (g, n) in enumerate(stages):
        for i in range(1, n):
            bulk_wait(vec_land.at[0], vec_s.at[stage, i])
            for half in range(2):
                bulk_wait(lands[stage].at[half, 0], rs_s.at[half, stage, i])
                bulk_wait(piece(half, stage, place[stage]), ag_s.at[half, stage, i])


def per_device(
    query_text_memory,
    query_text_feed,
    reply_acceptor_memory,
    reply_feed,
    reply_cotangent_vector,
    query_placement,
    reply_parent_query,
    fading_narrowing,
    fading_widening,
    fading_anchor_rate,
    self_emphasis,
    lagged_token_fraction,
):
    devices = lax.axis_size("dp")
    ranks = lax.axis_size("mp")
    channels = query_text_feed.shape[2]
    pairs = channels // LANES
    per = HEAD * pairs // devices
    responses = reply_parent_query.shape[0]
    matches = query_placement[None, :] == reply_parent_query[:, None]
    slots = jnp.arange(devices, dtype=jnp.int32)
    owner = jnp.sum(jnp.where(matches, slots[None, :], 0), axis=1).astype(jnp.int32)
    index = jnp.arange(responses, dtype=jnp.int32)
    index = (index + index // 2 + 1)[:, None]
    first = jnp.min(jnp.where(matches, index, 3 * responses), axis=0)
    last = jnp.max(jnp.where(matches, index, -1), axis=0)
    child = jnp.stack([first, last], axis=1).reshape(-1).astype(jnp.int32)
    gaps = gap_masks()
    stages = stages_of(devices)
    size = [channels]
    for g, n in stages:
        size.append(size[-1] // n)

    def vmem(*shape, dtype=F32):
        return pltpu.VMEM(shape, dtype)

    dma = pltpu.SemaphoreType.DMA
    scratch = [
        vmem(1, channels),
        vmem(devices, 1, channels),
        vmem(3 * T, channels),
        vmem(3 * T, RANK),
        vmem(ranks, 3 * T, RANK),
        vmem(8, channels),
        vmem(ranks, 8, RANK),
        vmem(3 * T, channels),
        vmem(3 * T, channels),
        vmem(devices, 3, per, LANES),
        vmem(3 * devices, per, LANES),
        vmem(devices, 3, per, LANES),
        vmem(devices, 3, per, LANES),
        vmem(2, T, channels),
        vmem(2, T, channels),
        vmem(3 * T, RANK),
        vmem(3 * T, channels),
        vmem(3 * T, RANK),
        vmem(ranks, 3 * T, RANK),
        vmem(8, RANK),
        vmem(devices, 8, RANK),
        vmem(9, 1, channels),
        vmem(sum(n for _, n in stages), 3, 1, channels),
        vmem(2, channels, RANK),
        vmem(2, size[1], RANK),
        vmem(2, size[2], RANK),
        vmem(2, size[3], RANK),
        vmem(2, stages[0][1], size[1], RANK),
        vmem(2, stages[1][1], size[2], RANK),
        vmem(2, stages[2][1], size[3], RANK),
        vmem(2, channels, RANK),
        dma,
        dma,
        dma((ranks,)),
        dma((ranks,)),
        dma((ranks,)),
        dma((ranks,)),
        dma,
        dma,
        dma,
        dma,
        dma((ranks,)),
        dma((ranks,)),
        dma,
        dma,
        dma((3, 8)),
        dma((3, 8)),
        dma((2, 3, 8)),
        dma((2, 3, 8)),
        dma((2, 3, 8)),
        dma((2, 3, 8)),
    ]
    whole = pl.BlockSpec(memory_space=pltpu.VMEM)
    scalars = pl.BlockSpec(memory_space=pltpu.SMEM)
    rkv, xr, kv, xp, down, up, vec = pl.pallas_call(
        functools.partial(body, devices, ranks, channels),
        out_shape=(
            jax.ShapeDtypeStruct(reply_acceptor_memory.shape, BF16),
            jax.ShapeDtypeStruct(reply_feed.shape, BF16),
            jax.ShapeDtypeStruct(query_text_memory.shape, BF16),
            jax.ShapeDtypeStruct(query_text_feed.shape, BF16),
            jax.ShapeDtypeStruct(fading_narrowing.shape, F32),
            jax.ShapeDtypeStruct(fading_widening.shape, F32),
            jax.ShapeDtypeStruct((3, 1, channels), F32),
        ),
        in_specs=[scalars] * 2 + [whole] * 13,
        out_specs=[whole] * 7,
        scratch_shapes=scratch,
        compiler_params=pltpu.CompilerParams(
            collective_id=0, has_side_effects=True, vmem_limit_bytes=48 * 1024 * 1024
        ),
    )(
        owner,
        child,
        query_text_memory,
        query_text_feed,
        reply_acceptor_memory,
        reply_feed,
        reply_cotangent_vector,
        fading_narrowing,
        fading_widening,
        fading_anchor_rate[None],
        self_emphasis[None],
        lagged_token_fraction[None],
        jnp.asarray(gaps, BF16),
        jnp.asarray(gaps.T, BF16),
        jnp.asarray(level_masks(), F32),
    )
    return rkv, xr, kv, xp, down, up, vec[0, 0], vec[1, 0], vec[2, 0]


def solution(mesh):
    in_specs = (
        P(None, "dp", None, "mp"),
        P("dp", None, "mp"),
        P(None, "dp", None, "mp"),
        P("dp", None, "mp"),
        P("dp", None, "mp"),
        P(),
        P(),
        P("mp", None),
        P(None, "mp"),
        P("mp"),
        P("mp"),
        P("mp"),
    )
    out_specs = (
        P(None, "dp", None, "mp"),
        P("dp", None, "mp"),
        P(None, "dp", None, "mp"),
        P("dp", None, "mp"),
        P("mp", None),
        P(None, "mp"),
        P("mp"),
        P("mp"),
        P("mp"),
    )
    return jax.shard_map(
        per_device, mesh=mesh, in_specs=in_specs, out_specs=out_specs, check_vma=False
    )
```

```python
import functools

import jax
import jax.numpy as jnp
from jax import lax
from jax.experimental import pallas as pl
from jax.experimental.pallas import tpu as pltpu
from jax.sharding import PartitionSpec as P

HEAD = 64
T = 64
LANES = 128
RANK = 128
VMEM = 63 * 1024 * 1024
LEVELS = (32, 16, 8, 4, 2, 1)
MESH = pl.DeviceIdType.MESH
F32 = jnp.float32
BF16 = jnp.bfloat16


def stages_of(devices):
    if devices == 64:
        return ((1, 2), (2, 4), (8, 8))
    return ((1, 2), (2, 2), (4, devices // 4))


def nn(a, b):
    return lax.dot_general(a, b, (((1,), (0,)), ((), ())), preferred_element_type=F32)


def nt(a, b):
    return lax.dot_general(a, b, (((1,), (1,)), ((), ())), preferred_element_type=F32)


def tn(a, b):
    return lax.dot_general(a, b, (((0,), (0,)), ((), ())), preferred_element_type=F32)


def split(x):
    hi = x.astype(BF16)
    return hi, (x - hi.astype(F32)).astype(BF16)


def split3(x):
    hi = x.astype(BF16)
    rest = x - hi.astype(F32)
    mid = rest.astype(BF16)
    return hi, mid, (rest - mid.astype(F32)).astype(BF16)


def dot3(dot, a, b):
    return dot(a[0], b[0]) + (dot(a[0], b[1]) + dot(a[1], b[0]))


def left2(dot, a, b):
    return dot(a[0], b) + dot(a[1], b)


def right2(dot, a, b):
    return dot(a, b[0]) + dot(a, b[1])


def lane_head(shape):
    return lax.broadcasted_iota(jnp.int32, shape, len(shape) - 1) < HEAD


def block_diag(x):
    low = lane_head(x.shape)
    zero = jnp.zeros_like(x)
    return jnp.concatenate([jnp.where(low, x, zero), jnp.where(low, zero, x)], axis=0)


def pack_diag(m):
    return jnp.where(lane_head((HEAD, LANES)), m[:HEAD], m[HEAD:])


def body(
    devices,
    ranks,
    channels,
    owner_ref,
    first_ref,
    last_ref,
    kv_hbm,
    xp_hbm,
    rkv_hbm,
    xr_hbm,
    dy_hbm,
    down_hbm,
    up_hbm,
    base_hbm,
    u_hbm,
    f_hbm,
    rkv_hbm_out,
    xr_hbm_out,
    kv_hbm_out,
    xp_hbm_out,
    grad_hbm_out,
    vec_hbm_out,
    rkv_out,
    xr_out,
    kv_out,
    xp_out,
    vec_out,
    kv_ref,
    xp_ref,
    rkv_ref,
    xr_ref,
    dy_ref,
    down_ref,
    up_ref,
    base_ref,
    u_ref,
    f_ref,
    gaps_ref,
    gaps_t_ref,
    masks_ref,
    row_src,
    row_land,
    mixed,
    hid_p,
    hid_p_land,
    hid_r,
    hid_r_land,
    lead,
    lead_hid,
    lead_land,
    dec,
    ef,
    send_f1,
    recv_f1,
    send_b1,
    recv_b1,
    send_f2,
    recv_f2,
    send_b2,
    recv_b2,
    dr_loc,
    dd_loc,
    th_ref,
    dz_ref,
    dth_r_src,
    dth_r_land,
    dth_p_src,
    dth_p_land,
    dh_ref,
    dh_land,
    xp_tail,
    vec,
    vec_land,
    grad,
    cur1,
    cur2,
    cur3,
    land0,
    land1,
    land2,
    fin,
    in_sem,
    out_sem,
    row_s,
    row_r,
    hid_p_s,
    hid_p_r,
    hid_r_s,
    hid_r_r,
    lead_s,
    lead_r,
    route_s,
    route_r,
    dth_r_s,
    dth_r_r,
    dth_p_s,
    dth_p_r,
    dh_s,
    dh_r,
    vec_s,
    vec_r,
    rs_s,
    rs_r,
    ag_s,
    ag_r,
):
    me = lax.axis_index("dp")
    rank = lax.axis_index("mp")
    pairs = channels // LANES
    per = HEAD * pairs // devices
    dests = HEAD // per
    stages = stages_of(devices)

    def lanes(p):
        return pl.ds(pl.multiple_of(p * LANES, LANES), LANES)

    rows_of = lanes

    def loop(n, fn, init=None):
        if init is None:
            lax.fori_loop(0, n, lambda i, c: (fn(i), c)[1], 0)
            return None
        return lax.fori_loop(0, n, fn, init)

    def remote(src, dst, ssem, rsem, axis, peer):
        return pltpu.make_async_remote_copy(
            src_ref=src,
            dst_ref=dst,
            send_sem=ssem,
            recv_sem=rsem,
            device_id={axis: peer},
            device_id_type=MESH,
        )

    def bulk_wait(view, sem):
        pltpu.make_async_copy(view, view, sem).wait()

    barrier = pltpu.get_barrier_semaphore()

    def greet(i):
        pl.semaphore_signal(
            barrier, inc=1, device_id={"dp": lax.rem(me + 1 + i, devices)}, device_id_type=MESH
        )

    for i in range(1, ranks):
        pl.semaphore_signal(
            barrier, inc=1, device_id={"mp": lax.rem(rank + i, ranks)}, device_id_type=MESH
        )
    loop(devices - 1, greet)

    fetches = [
        pltpu.make_async_copy(src, dst, in_sem.at[n])
        for n, (src, dst) in enumerate(
            (
                (xp_hbm, xp_ref),
                (xr_hbm, xr_ref),
                (f_hbm, f_ref),
                (down_hbm, down_ref),
                (up_hbm, up_ref),
                (base_hbm, base_ref),
                (kv_hbm, kv_ref),
                (rkv_hbm, rkv_ref),
                (dy_hbm, dy_ref),
                (u_hbm, u_ref),
            )
        )
    ]
    for fetch in fetches:
        fetch.start()

    stores = []

    def store(src, dst):
        copy = pltpu.make_async_copy(src, dst, out_sem.at[len(stores)])
        copy.start()
        stores.append(copy)

    def gap_mask(shape, t_axis, level):
        t = lax.broadcasted_iota(jnp.int32, shape, t_axis)
        j = lax.broadcasted_iota(jnp.int32, shape, 1 - t_axis)
        if level == len(LEVELS):
            return (j < t).astype(F32).astype(BF16)
        b = LEVELS[level]
        second = (t & b) != 0
        late = second & (j >= (t & -b)) & (j < t)
        early = ~second & (j > t) & (j <= (t | (b - 1)))
        return (late | early).astype(F32).astype(BF16)

    for level in range(len(LEVELS) + 1):
        gaps_ref[level * T : (level + 1) * T, :] = gap_mask((T, T), 0, level)
    for level in range(0, len(LEVELS), 2):
        both = [gap_mask((T, T), 1, level + n) for n in range(2)]
        gaps_t_ref[:, level * T : (level + 2) * T] = jnp.concatenate(both, axis=1)
    t_row = lax.broadcasted_iota(jnp.int32, (T, LANES), 0)
    s_col = lax.broadcasted_iota(jnp.int32, (T, LANES), 1) & (T - 1)
    apart = t_row ^ s_col
    for level, b in enumerate(LEVELS):
        masks_ref[level * T : (level + 1) * T, :] = ((apart >= b) & (apart < 2 * b)).astype(F32)

    first_row = lax.broadcasted_iota(jnp.int32, (T, LANES), 0) == 0
    last_row = lax.broadcasted_iota(jnp.int32, (T, LANES), 0) == T - 1

    def x_of(i, p):
        return (xp_ref[0, :, lanes(p)] if i == 0 else xr_ref[i - 1, :, lanes(p)]).astype(F32)

    def mix(p, acc):
        f = f_ref[:, lanes(p)]
        parts = []
        for i in range(3):
            x = x_of(i, p)
            prev = jnp.where(first_row, 0.0, pltpu.roll(x, 1, 0))
            m = x + (prev - x) * f
            mixed[i * T : (i + 1) * T, lanes(p)] = m
            parts.append(m)
        return acc + dot3(nn, split(jnp.concatenate(parts, axis=0)), split(down_ref[rows_of(p), :]))

    for fetch in fetches[:4]:
        fetch.wait()
    row_src[...] = xp_ref[0, T - 16 :, :].astype(F32)[15:16]
    partial = loop(pairs, mix, jnp.zeros((3 * T, RANK), F32))
    hid_p[...] = partial[:T]
    hid_r[...] = partial[T:]
    for fetch in fetches[4:]:
        fetch.wait()
    pl.semaphore_wait(barrier, devices - 1 + ranks - 1)

    def exchange(src, land, ssem, rsem):
        for i in range(1, ranks):
            peer = lax.rem(rank + i, ranks)
            remote(src, land.at[rank], ssem.at[i], rsem.at[rank], "mp", peer).start()
        land[rank] = src[...]

    def exchanged(land, rsem):
        for i in range(1, ranks):
            source = lax.rem(rank + i, ranks)
            bulk_wait(land.at[source], rsem.at[source])
        total = land[0]
        for i in range(1, ranks):
            total = total + land[i]
        return total

    def send_row(i):
        peer = lax.rem(me + 1 + i, devices)
        remote(row_src, row_land.at[me], row_s, row_r, "dp", peer).start()

    exchange(hid_p, hid_p_land, hid_p_s, hid_p_r)
    loop(devices - 1, send_row)
    row_land[me] = row_src[...]
    exchange(hid_r, hid_r_land, hid_r_s, hid_r_r)
    before = gaps_ref[len(LEVELS) * T :, :]
    suffix = (
        lax.broadcasted_iota(jnp.int32, (T, T), 1) > lax.broadcasted_iota(jnp.int32, (T, T), 0)
    ).astype(F32).astype(BF16)

    def exact(mask, x):
        hi, mid, low = split3(x)
        return nn(mask, hi) + (nn(mask, mid) + nn(mask, low))

    def decays(lo, hi, p):
        z = dot3(nn, split(th_ref[lo * T : hi * T, :]), split(up_ref[:, lanes(p)]))
        d = -jnp.exp(z + base_ref[:, lanes(p)])
        dec[lo * T : hi * T, lanes(p)] = d
        for i in range(lo, hi):
            at = (i - lo) * T
            e = jnp.exp(exact(suffix if i == 0 else before, d[at : at + T]))
            ef[i * T : (i + 1) * T, lanes(p)] = e
            if i == 0:
                a, b = kv_ref[0, 0, :, lanes(p)], kv_ref[1, 0, :, lanes(p)]
            else:
                a, b = rkv_ref[0, i - 1, :, lanes(p)], dy_ref[i - 1, :, lanes(p)]
            packed = pack_diag(left2(tn, split(a.astype(F32) * e), b)).reshape(dests, per, LANES)
            if i == 0:
                send_f1[pl.ds(p * dests, dests)] = packed
            else:
                send_b1[pl.ds(p * dests, dests), i - 1] = packed

    def route(n, src, dst_of):
        def send(i):
            peer = lax.rem(me + 1 + i, devices)
            remote(src.at[peer], dst_of(me), route_s.at[n], route_r.at[n], "dp", peer).start()

        loop(devices - 1, send)

    th_ref[:T, :] = jnp.tanh(exchanged(hid_p_land, hid_p_r))
    loop(pairs, functools.partial(decays, 0, 1))
    route(0, send_f1, lambda m: recv_f1.at[m])
    recv_f1[me] = send_f1[me]

    bulk_wait(row_land.at[pl.ds(0, devices - 1)], row_r)
    lead_rows = [row_land[owner_ref[2 * me + i]] for i in range(2)]
    row8 = lax.broadcasted_iota(jnp.int32, (8, channels), 0)
    lead[...] = jnp.where(row8 == 0, lead_rows[0], jnp.where(row8 == 1, lead_rows[1], 0.0))

    def lead_mix(p, acc):
        fl = f_ref[:, lanes(p)] * lead[:, lanes(p)]
        for i in range(2):
            at = (i + 1) * T
            mixed[at : at + 1, lanes(p)] = mixed[at : at + 1, lanes(p)] + fl[i : i + 1]
        return acc + dot3(nn, split(fl), split(down_ref[rows_of(p), :]))

    lead_hid[...] = loop(pairs, lead_mix, jnp.zeros((8, RANK), F32))
    exchange(lead_hid, lead_land, lead_s, lead_r)
    hidden = exchanged(hid_r_land, hid_r_r)
    th_ref[T:, :] = jnp.tanh(hidden)
    extra = exchanged(lead_land, lead_r)
    for i in range(2):
        at = (i + 1) * T
        th_ref[at : at + 1, :] = jnp.tanh(hidden[i * T : i * T + 1] + extra[i : i + 1])
    loop(pairs, functools.partial(decays, 1, 3))
    route(1, send_b1, lambda m: recv_b1.at[pl.ds(2 * m, 2)])
    recv_b1[pl.ds(2 * me, 2)] = send_b1[me]

    bulk_wait(recv_f1.at[pl.ds(0, devices - 1)], route_r.at[0])

    def shuffle_f(n):
        send_f2[n, 0] = recv_f1[owner_ref[2 * n]]
        send_f2[n, 1] = recv_f1[owner_ref[2 * n + 1]]

    loop(devices, shuffle_f)
    route(2, send_f2, lambda m: recv_f2.at[m])
    recv_f2[me] = send_f2[me]

    ones_block = (
        (
            (lax.broadcasted_iota(jnp.int32, (LANES, LANES), 0) < HEAD)
            == (lax.broadcasted_iota(jnp.int32, (LANES, LANES), 1) < HEAD)
        )
        .astype(F32)
        .astype(BF16)
    )

    def inner(i, p):
        rb, kb, vb = (rkv_ref[n, i, :, lanes(p)] for n in range(3))
        yb = dy_ref[i, :, lanes(p)]
        r, k, v, y = (a.astype(F32) for a in (rb, kb, vb, yb))
        d = dec[(i + 1) * T : (i + 2) * T, lanes(p)]
        u = u_ref[:, lanes(p)]
        y_diag = block_diag(yb)
        sym = jnp.where(t_row > s_col, nt(yb, block_diag(vb)), nt(vb, y_diag))
        gap = exact(gaps_ref[: len(LEVELS) * T, :], d)
        att = jnp.zeros((T, LANES), F32)
        dr = jnp.zeros((T, LANES), F32)
        dk = jnp.zeros((T, LANES), F32)
        dgaps = []
        for level, b in enumerate(LEVELS):
            second = (t_row & b) != 0
            mask = masks_ref[level * T : (level + 1) * T, :]
            x = jnp.exp(gap[level * T : (level + 1) * T])
            w = jnp.where(second, r, k) * x
            ws = split(w)
            wd = tuple(block_diag(a) for a in ws)
            att = att + mask * dot3(nt, ws, wd)
            dw = dot3(nn, split(mask * sym), wd)
            dgaps.append(w * dw)
            g = x * dw
            dr = dr + jnp.where(second, g, 0.0)
            dk = dk + jnp.where(second, 0.0, g)
        dgap = jnp.concatenate(dgaps, axis=0)
        dd_loc[i, :, lanes(p)] = right2(nn, gaps_t_ref[...], split(dgap))
        self_a = left2(nn, split(r * u * k), ones_block)
        self_b = left2(nn, split(y * v), ones_block)
        dv = left2(nn, split(jnp.where(s_col > t_row, att, 0.0)), y_diag) + self_a * y
        dr_loc[i, :, lanes(p)] = dr + u * k * self_b
        rkv_out[1, i, :, lanes(p)] = (dk + u * r * self_b).astype(BF16)
        rkv_out[2, i, :, lanes(p)] = dv.astype(BF16)
        part = jnp.sum(r * k * self_b, axis=0, keepdims=True)
        if i == 0:
            vec[1, :, lanes(p)] = part
        else:
            vec[1, :, lanes(p)] = vec[1, :, lanes(p)] + part

    loop(pairs, functools.partial(inner, 0))
    bulk_wait(recv_b1.at[pl.ds(0, 2 * (devices - 1))], route_r.at[1])

    def shuffle_b(n):
        send_b2[n] = recv_b1[first_ref[n]] + recv_b1[last_ref[n]]

    loop(devices, shuffle_b)
    route(3, send_b2, lambda m: recv_b2.at[m])
    recv_b2[me] = send_b2[me]
    loop(pairs, functools.partial(inner, 1))

    def outer_r(p):
        for i in range(2):
            state = recv_f2[pl.ds(p * dests, dests), i].reshape(HEAD, LANES)
            sd = tuple(block_diag(a) for a in split(state))
            rows = slice((i + 1) * T, (i + 2) * T)
            r = rkv_ref[0, i, :, lanes(p)].astype(F32)
            drs = ef[rows, lanes(p)] * right2(nt, dy_ref[i, :, lanes(p)], sd)
            rkv_out[0, i, :, lanes(p)] = (dr_loc[i, :, lanes(p)] + drs).astype(BF16)
            dd = right2(nn, suffix, split(r * drs)) + dd_loc[i, :, lanes(p)]
            dz_ref[rows, lanes(p)] = dd * dec[rows, lanes(p)]

    def outer_p(p):
        state = recv_b2[pl.ds(p * dests, dests)].reshape(HEAD, LANES)
        sd = tuple(block_diag(a) for a in split(state))
        e = ef[:T, lanes(p)]
        k = kv_ref[0, 0, :, lanes(p)].astype(F32)
        dk = e * right2(nt, kv_ref[1, 0, :, lanes(p)], sd)
        dv = dot3(nn, split(k * e), sd)
        kv_out[0, 0, :, lanes(p)] = dk.astype(BF16)
        kv_out[1, 0, :, lanes(p)] = dv.astype(BF16)
        dd = right2(nn, before, split(k * dk))
        dz_ref[:T, lanes(p)] = dd * dec[:T, lanes(p)]

    def dth_part(lo, hi, p, acc):
        return acc + dot3(nt, split(dz_ref[lo * T : hi * T, lanes(p)]), split(up_ref[:, lanes(p)]))

    bulk_wait(recv_f2.at[pl.ds(0, devices - 1)], route_r.at[2])
    loop(pairs, outer_r)
    dth_r_src[...] = loop(
        pairs, functools.partial(dth_part, 1, 3), jnp.zeros((2 * T, RANK), F32)
    )
    exchange(dth_r_src, dth_r_land, dth_r_s, dth_r_r)
    bulk_wait(recv_b2.at[pl.ds(0, devices - 1)], route_r.at[3])
    loop(pairs, outer_p)
    dth_p_src[...] = loop(pairs, functools.partial(dth_part, 0, 1), jnp.zeros((T, RANK), F32))
    exchange(dth_p_src, dth_p_land, dth_p_s, dth_p_r)
    store(rkv_out, rkv_hbm_out)
    store(kv_out, kv_hbm_out)

    place = [lax.rem(me // g, n) for g, n in stages]
    size = [channels]
    for g, n in stages:
        size.append(size[-1] // n)
    lands = (land0, land1, land2)
    sums = (cur1, cur2, cur3)

    def peers(stage):
        g, n = stages[stage]
        q = place[stage]
        for i in range(1, n):
            other = lax.rem(q + i, n)
            yield i, other, me + (other - q) * g

    def source(half, stage):
        return grad.at[half] if stage == 0 else sums[stage - 1].at[half]

    def rs_start(half, stage):
        rows = size[stage + 1]
        for i, other, peer in peers(stage):
            remote(
                source(half, stage).at[pl.ds(pl.multiple_of(other * rows, 8), rows)],
                lands[stage].at[half, place[stage]],
                rs_s.at[half, stage, i],
                rs_r.at[half, stage, place[stage]],
                "dp",
                peer,
            ).start()

    def rs_finish(half, stage):
        rows = size[stage + 1]
        total = source(half, stage)[pl.ds(pl.multiple_of(place[stage] * rows, 8), rows), :]
        for i, other, peer in peers(stage):
            bulk_wait(lands[stage].at[half, other], rs_r.at[half, stage, other])
            total = total + lands[stage][half, other]
        sums[stage][half] = total

    offs = [0]
    for stage in range(3):
        offs.append(offs[-1] + place[stage] * size[stage + 1])

    def piece(half, stage, q):
        rows = size[stage + 1]
        return fin.at[half, pl.ds(pl.multiple_of(offs[stage] + q * rows, 8), rows)]

    def ag_start(half, stage):
        if stage == 2:
            fin[half, pl.ds(pl.multiple_of(offs[3], 8), size[3]), :] = sums[2][half]
        q = place[stage]
        mine = piece(half, stage, q)
        for i, other, peer in peers(stage):
            ssem, rsem = ag_s.at[half, stage, i], ag_r.at[half, stage, q]
            remote(mine, mine, ssem, rsem, "dp", peer).start()

    def ag_finish(half, stage):
        for i, other, peer in peers(stage):
            bulk_wait(piece(half, stage, other), ag_r.at[half, stage, other])

    def vec_start(stage):
        q = place[stage]
        at = sum(m for _, m in stages[:stage])
        mine = vec.at[pl.ds(3 * stage, 3)]
        for i, other, peer in peers(stage):
            ssem, rsem = vec_s.at[stage, i], vec_r.at[stage, q]
            remote(mine, vec_land.at[at + q], ssem, rsem, "dp", peer).start()
        vec_land[at + q] = vec[3 * stage : 3 * stage + 3]

    def vec_finish(stage):
        at = sum(m for _, m in stages[:stage])
        for i, other, peer in peers(stage):
            bulk_wait(vec_land.at[at + other], vec_r.at[stage, other])
        total = vec_land[at]
        for i in range(1, stages[stage][1]):
            total = total + vec_land[at + i]
        if stage == 2:
            vec_out[...] = total
        else:
            vec[3 * stage + 3 : 3 * stage + 6] = total

    def dh_piece(stage, q):
        g = stages[stage][0]
        return dh_land.at[pl.ds(2 * (me - lax.rem(me, g) + (q - place[stage]) * g), 2 * g)]

    def dh_start(stage):
        q = place[stage]
        mine = dh_piece(stage, q)
        for i, other, peer in peers(stage):
            remote(mine, mine, dh_s.at[stage, i], dh_r.at[stage, q], "dp", peer).start()

    def dh_finish(stage):
        for i, other, peer in peers(stage):
            bulk_wait(dh_piece(stage, other), dh_r.at[stage, other])

    def up_grads(p):
        dz = dz_ref[:, lanes(p)]
        grad[0, rows_of(p), :] = dot3(tn, split(th_ref[...]), split(dz))
        vec[0, :, lanes(p)] = jnp.sum(dz, axis=0, keepdims=True)

    loop(pairs, up_grads)
    rs_start(0, 0)

    th = th_ref[T:, :]
    dh_ref[T:, :] = exchanged(dth_r_land, dth_r_r) * (1.0 - th * th)
    for i in range(2):
        dh_land[2 * me + i] = dh_ref[(i + 1) * T : (i + 1) * T + 1, :]
    dh_start(0)
    th = th_ref[:T, :]
    dh_ref[:T, :] = exchanged(dth_p_land, dth_p_r) * (1.0 - th * th)

    def down_grads(p):
        grad[1, rows_of(p), :] = dot3(tn, split(mixed[:, lanes(p)]), split(dh_ref[...]))

    loop(pairs, down_grads)
    rs_start(1, 0)

    def x_grads(p):
        f = f_ref[:, lanes(p)]
        dm = dot3(nt, split(dh_ref[...]), split(down_ref[rows_of(p), :]))
        mix_sum = jnp.zeros((1, LANES), F32)
        for i in range(3):
            x = x_of(i, p)
            g = dm[i * T : (i + 1) * T]
            ahead = jnp.where(last_row, 0.0, pltpu.roll(g, T - 1, 0))
            first = 0.0 if i == 0 else lead[i - 1 : i, lanes(p)]
            prev = jnp.where(first_row, first, pltpu.roll(x, 1, 0))
            dx = g + (ahead - g) * f
            mix_sum = mix_sum + jnp.sum(g * (prev - x), axis=0, keepdims=True)
            if i == 0:
                xp_out[0, :, lanes(p)] = dx.astype(BF16)
                xp_tail[:, lanes(p)] = dx[T - 16 :]
            else:
                xr_out[i - 1, :, lanes(p)] = dx.astype(BF16)
        vec[2, :, lanes(p)] = mix_sum

    def x_tail(late, p):
        f = f_ref[:, lanes(p)]
        more = f * dot3(nt, split(late), split(down_ref[rows_of(p), :]))[0:1]
        tail = xp_tail[:, lanes(p)]
        at_end = lax.broadcasted_iota(jnp.int32, (16, LANES), 0) == 15
        xp_out[0, T - 16 :, lanes(p)] = jnp.where(at_end, tail + more, tail).astype(BF16)

    rs_finish(0, 0)
    rs_start(0, 1)
    dh_finish(0)
    dh_start(1)
    loop(pairs, x_grads)
    vec_start(0)
    store(xr_out, xr_hbm_out)
    rs_finish(1, 0)
    rs_start(1, 1)
    rs_finish(0, 1)
    rs_start(0, 2)
    dh_finish(1)
    dh_start(2)
    vec_finish(0)
    vec_start(1)
    rs_finish(1, 1)
    rs_start(1, 2)
    rs_finish(0, 2)
    ag_start(0, 2)
    vec_finish(1)
    vec_start(2)
    rs_finish(1, 2)
    ag_start(1, 2)
    dh_finish(2)
    late = dh_land[first_ref[me]] + dh_land[last_ref[me]]
    loop(pairs, functools.partial(x_tail, jnp.broadcast_to(late, (8, RANK))))
    store(xp_out, xp_hbm_out)
    ag_finish(0, 2)
    ag_start(0, 1)
    vec_finish(2)
    store(vec_out, vec_hbm_out)
    ag_finish(1, 2)
    ag_start(1, 1)
    ag_finish(0, 1)
    ag_start(0, 0)
    ag_finish(1, 1)
    ag_start(1, 0)
    ag_finish(0, 0)
    store(fin.at[0], grad_hbm_out.at[0])
    ag_finish(1, 0)
    store(fin.at[1], grad_hbm_out.at[1])

    bulk_wait(row_land.at[pl.ds(0, devices - 1)], row_s)
    bulk_wait(recv_f1.at[pl.ds(0, devices - 1)], route_s.at[0])
    bulk_wait(recv_b1.at[pl.ds(0, 2 * (devices - 1))], route_s.at[1])
    bulk_wait(recv_f2.at[pl.ds(0, devices - 1)], route_s.at[2])
    bulk_wait(recv_b2.at[pl.ds(0, devices - 1)], route_s.at[3])
    for i in range(1, ranks):
        bulk_wait(hid_p_land.at[0], hid_p_s.at[i])
        bulk_wait(hid_r_land.at[0], hid_r_s.at[i])
        bulk_wait(lead_land.at[0], lead_s.at[i])
        bulk_wait(dth_r_land.at[0], dth_r_s.at[i])
        bulk_wait(dth_p_land.at[0], dth_p_s.at[i])
    for stage, (g, n) in enumerate(stages):
        for i in range(1, n):
            bulk_wait(vec_land.at[0], vec_s.at[stage, i])
            bulk_wait(dh_piece(stage, place[stage]), dh_s.at[stage, i])
            for half in range(2):
                bulk_wait(lands[stage].at[half, 0], rs_s.at[half, stage, i])
                bulk_wait(piece(half, stage, place[stage]), ag_s.at[half, stage, i])
    for copy in stores:
        copy.wait()


def results(pairs, *refs):
    sources, outs, held, (in_sem, out_sem) = refs[:6], refs[6:15], refs[15:21], refs[21:]
    loads = [
        pltpu.make_async_copy(a, b, in_sem.at[n]) for n, (a, b) in enumerate(zip(sources, held))
    ]
    for load in loads:
        load.start()
    moves = [[(held[n], outs[n])] for n in range(4)]
    moves.append([(held[4].at[1], outs[4])])
    for p in range(pairs):
        lanes = pl.ds(p * LANES, LANES)
        moves[4].append((held[4].at[0, lanes], outs[5].at[:, lanes]))
    moves.append([(held[5].at[n], outs[6 + n]) for n in range(3)])
    copies = []
    for load, group in zip(loads, moves):
        load.wait()
        for src, dst in group:
            copies.append(pltpu.make_async_copy(src, dst, out_sem.at[len(copies)]))
            copies[-1].start()
    for copy in copies:
        copy.wait()


def per_device(
    query_text_memory,
    query_text_feed,
    reply_acceptor_memory,
    reply_feed,
    reply_cotangent_vector,
    query_placement,
    reply_parent_query,
    fading_narrowing,
    fading_widening,
    fading_anchor_rate,
    self_emphasis,
    lagged_token_fraction,
):
    devices = lax.axis_size("dp")
    ranks = lax.axis_size("mp")
    channels = query_text_feed.shape[2]
    pairs = channels // LANES
    per = HEAD * pairs // devices
    responses = reply_parent_query.shape[0]
    matches = query_placement[None, :] == reply_parent_query[:, None]
    slots = jnp.arange(devices, dtype=jnp.int32)
    owner = jnp.sum(jnp.where(matches, slots[None, :], 0), axis=1).astype(jnp.int32)
    index = jnp.arange(responses, dtype=jnp.int32)[:, None]
    first = jnp.min(jnp.where(matches, index, responses - 1), axis=0)
    last = jnp.max(jnp.where(matches, index, 0), axis=0)
    stages = stages_of(devices)
    size = [channels]
    for g, n in stages:
        size.append(size[-1] // n)

    def vmem(*shape, dtype=F32):
        return pltpu.VMEM(shape, dtype)

    operands = (
        query_text_memory,
        query_text_feed,
        reply_acceptor_memory,
        reply_feed,
        reply_cotangent_vector,
        fading_narrowing,
        fading_widening,
        fading_anchor_rate[None],
        self_emphasis[None],
        lagged_token_fraction[None],
    )
    dma = pltpu.SemaphoreType.DMA
    shapes = [
        jax.ShapeDtypeStruct(a.shape, BF16)
        for a in (reply_acceptor_memory, reply_feed, query_text_memory, query_text_feed)
    ]
    scratch = [pltpu.VMEM(a.shape, a.dtype) for a in shapes]
    scratch += [vmem(3, 1, channels)]
    scratch += [pltpu.VMEM(a.shape, a.dtype) for a in operands]
    scratch += [
        vmem((len(LEVELS) + 1) * T, T, dtype=BF16),
        vmem(T, len(LEVELS) * T, dtype=BF16),
        vmem(len(LEVELS) * T, LANES),
        vmem(1, channels),
        vmem(devices, 1, channels),
        vmem(3 * T, channels),
        vmem(T, RANK),
        vmem(ranks, T, RANK),
        vmem(2 * T, RANK),
        vmem(ranks, 2 * T, RANK),
        vmem(8, channels),
        vmem(8, RANK),
        vmem(ranks, 8, RANK),
        vmem(3 * T, channels),
        vmem(3 * T, channels),
        vmem(devices, per, LANES),
        vmem(devices, per, LANES),
        vmem(devices, 2, per, LANES),
        vmem(2 * devices, per, LANES),
        vmem(devices, 2, per, LANES),
        vmem(devices, 2, per, LANES),
        vmem(devices, per, LANES),
        vmem(devices, per, LANES),
        vmem(2, T, channels),
        vmem(2, T, channels),
        vmem(3 * T, RANK),
        vmem(3 * T, channels),
        vmem(2 * T, RANK),
        vmem(ranks, 2 * T, RANK),
        vmem(T, RANK),
        vmem(ranks, T, RANK),
        vmem(3 * T, RANK),
        vmem(2 * devices, 1, RANK),
        vmem(16, channels),
        vmem(9, 1, channels),
        vmem(sum(n for _, n in stages), 3, 1, channels),
        vmem(2, channels, RANK),
        vmem(2, size[1], RANK),
        vmem(2, size[2], RANK),
        vmem(2, size[3], RANK),
        vmem(2, stages[0][1], size[1], RANK),
        vmem(2, stages[1][1], size[2], RANK),
        vmem(2, stages[2][1], size[3], RANK),
        vmem(2, channels, RANK),
        dma((len(operands),)),
        dma((7,)),
        dma,
        dma,
        dma((ranks,)),
        dma((ranks,)),
        dma((ranks,)),
        dma((ranks,)),
        dma((ranks,)),
        dma((ranks,)),
        dma((4,)),
        dma((4,)),
        dma((ranks,)),
        dma((ranks,)),
        dma((ranks,)),
        dma((ranks,)),
        dma((3, 8)),
        dma((3, 8)),
        dma((3, 8)),
        dma((3, 8)),
        dma((2, 3, 8)),
        dma((2, 3, 8)),
        dma((2, 3, 8)),
        dma((2, 3, 8)),
    ]
    scalars = pl.BlockSpec(memory_space=pltpu.SMEM)
    far = pl.BlockSpec(memory_space=pltpu.HBM)
    moved = pl.pallas_call(
        functools.partial(body, devices, ranks, channels),
        out_shape=(
            *shapes,
            jax.ShapeDtypeStruct((2, channels, RANK), F32),
            jax.ShapeDtypeStruct((3, 1, channels), F32),
        ),
        in_specs=[scalars] * 3 + [far] * len(operands),
        out_specs=[far] * 6,
        scratch_shapes=scratch,
        compiler_params=pltpu.CompilerParams(
            collective_id=0, has_side_effects=True, vmem_limit_bytes=VMEM
        ),
    )(owner, first, last, *operands)
    rkv, xr, kv, xp, down, up, *vectors = pl.pallas_call(
        functools.partial(results, pairs),
        out_shape=(
            *shapes,
            jax.ShapeDtypeStruct(fading_narrowing.shape, F32),
            jax.ShapeDtypeStruct(fading_widening.shape, F32),
            *[jax.ShapeDtypeStruct((1, channels), F32)] * 3,
        ),
        in_specs=[far] * 6,
        out_specs=[far] * 9,
        scratch_shapes=[pltpu.VMEM(a.shape, a.dtype) for a in moved]
        + [dma((6,)), dma((8 + pairs,))],
        compiler_params=pltpu.CompilerParams(vmem_limit_bytes=VMEM),
    )(*moved)
    return rkv, xr, kv, xp, down, up, *[v.reshape(channels) for v in vectors]


def solution(mesh):
    in_specs = (
        P(None, "dp", None, "mp"),
        P("dp", None, "mp"),
        P(None, "dp", None, "mp"),
        P("dp", None, "mp"),
        P("dp", None, "mp"),
        P(),
        P(),
        P("mp", None),
        P(None, "mp"),
        P("mp"),
        P("mp"),
        P("mp"),
    )
    out_specs = (
        P(None, "dp", None, "mp"),
        P("dp", None, "mp"),
        P(None, "dp", None, "mp"),
        P("dp", None, "mp"),
        P("mp", None),
        P(None, "mp"),
        P("mp"),
        P("mp"),
        P("mp"),
    )
    return jax.shard_map(
        per_device, mesh=mesh, in_specs=in_specs, out_specs=out_specs, check_vma=False
    )
```

```python
import functools

import jax
import jax.numpy as jnp
from jax import lax
from jax.experimental import pallas as pl
from jax.experimental.pallas import tpu as pltpu
from jax.sharding import PartitionSpec as P

HEAD = 64
T = 64
LANES = 128
RANK = 128
VMEM = 63 * 1024 * 1024
LEVELS = (32, 16, 8, 4, 2, 1)
MESH = pl.DeviceIdType.MESH
F32 = jnp.float32
BF16 = jnp.bfloat16


def stages_of(devices):
    if devices == 64:
        return ((1, 2), (2, 4), (8, 8))
    return ((1, 2), (2, 2), (4, devices // 4))


def nn(a, b):
    return lax.dot_general(a, b, (((1,), (0,)), ((), ())), preferred_element_type=F32)


def nt(a, b):
    return lax.dot_general(a, b, (((1,), (1,)), ((), ())), preferred_element_type=F32)


def tn(a, b):
    return lax.dot_general(a, b, (((0,), (0,)), ((), ())), preferred_element_type=F32)


def split(x):
    hi = x.astype(BF16)
    return hi, (x - hi.astype(F32)).astype(BF16)


def split3(x):
    hi = x.astype(BF16)
    rest = x - hi.astype(F32)
    mid = rest.astype(BF16)
    return hi, mid, (rest - mid.astype(F32)).astype(BF16)


def dot3(dot, a, b):
    return dot(a[0], b[0]) + (dot(a[0], b[1]) + dot(a[1], b[0]))


def left2(dot, a, b):
    return dot(a[0], b) + dot(a[1], b)


def right2(dot, a, b):
    return dot(a, b[0]) + dot(a, b[1])


def block_diag(x):
    head = lax.broadcasted_iota(jnp.int32, x.shape, 1) // HEAD
    zero = jnp.zeros_like(x)
    return jnp.concatenate(
        [jnp.where(head == h, x, zero) for h in range(x.shape[1] // HEAD)], axis=0
    )


def pack_diag(m):
    n = m.shape[1] // HEAD
    head = lax.broadcasted_iota(jnp.int32, (HEAD, m.shape[1]), 1) // HEAD
    out = m[:HEAD]
    for h in range(1, n):
        out = jnp.where(head == h, m[h * HEAD : (h + 1) * HEAD], out)
    return out


def body(
    devices,
    ranks,
    channels,
    place_hbm,
    parent_hbm,
    kv_hbm,
    xp_hbm,
    rkv_hbm,
    xr_hbm,
    dy_hbm,
    down_hbm,
    up_hbm,
    base_hbm,
    u_hbm,
    f_hbm,
    rkv_hbm_out,
    xr_hbm_out,
    kv_hbm_out,
    xp_hbm_out,
    grad_hbm_out,
    vec_hbm_out,
    rkv_out,
    xr_out,
    kv_out,
    xp_out,
    vec_out,
    place_ref,
    parent_ref,
    kv_ref,
    xp_ref,
    rkv_ref,
    xr_ref,
    dy_ref,
    down_ref,
    up_ref,
    base_ref,
    u_ref,
    f_ref,
    owner_vec,
    first_vec,
    last_vec,
    owner_ref,
    first_ref,
    last_ref,
    gaps_ref,
    gaps_t_ref,
    masks_ref,
    row_src,
    row_land,
    mixed,
    hid_p,
    hid_p_land,
    hid_r,
    hid_r_land,
    lead,
    lead_hid,
    lead_land,
    dec,
    ef,
    send_f1,
    recv_f1,
    send_b1,
    recv_b1,
    send_f2,
    recv_f2,
    send_b2,
    recv_b2,
    dr_loc,
    dd_loc,
    th_ref,
    dz_ref,
    dth_r_src,
    dth_r_land,
    dth_p_src,
    dth_p_land,
    dh_ref,
    dh_land,
    xp_tail,
    vec,
    vec_land,
    grad,
    cur1,
    cur2,
    cur3,
    land0,
    land1,
    land2,
    fin,
    in_sem,
    index_sem,
    out_sem,
    row_s,
    row_r,
    hid_p_s,
    hid_p_r,
    hid_r_s,
    hid_r_r,
    lead_s,
    lead_r,
    route_s,
    route_r,
    dth_r_s,
    dth_r_r,
    dth_p_s,
    dth_p_r,
    dh_s,
    dh_r,
    vec_s,
    vec_r,
    rs_s,
    rs_r,
    ag_s,
    ag_r,
):
    me = lax.axis_index("dp")
    rank = lax.axis_index("mp")
    wide = min(2 * LANES, channels)
    blocks = wide // LANES
    steps = channels // wide
    per = HEAD * (channels // LANES) // devices
    dests = HEAD // per
    stages = stages_of(devices)

    def lanes(p):
        return pl.ds(pl.multiple_of(p * wide, LANES), wide)

    rows_of = lanes

    def loop(n, fn, init=None):
        if init is None:
            lax.fori_loop(0, n, lambda i, c: (fn(i), c)[1], 0)
            return None
        return lax.fori_loop(0, n, fn, init)

    def remote(src, dst, ssem, rsem, axis, peer):
        return pltpu.make_async_remote_copy(
            src_ref=src,
            dst_ref=dst,
            send_sem=ssem,
            recv_sem=rsem,
            device_id={axis: peer},
            device_id_type=MESH,
        )

    def bulk_wait(view, sem):
        pltpu.make_async_copy(view, view, sem).wait()

    pending = []

    barrier = pltpu.get_barrier_semaphore()

    def greet(i):
        pl.semaphore_signal(
            barrier, inc=1, device_id={"dp": lax.rem(me + 1 + i, devices)}, device_id_type=MESH
        )

    fetches = [
        pltpu.make_async_copy(src, dst, in_sem.at[n])
        for n, (src, dst) in enumerate(
            (
                (xp_hbm, xp_ref),
                (xr_hbm, xr_ref),
                (f_hbm, f_ref),
                (down_hbm, down_ref),
                (up_hbm, up_ref),
                (base_hbm, base_ref),
                (kv_hbm, kv_ref),
                (rkv_hbm, rkv_ref),
                (dy_hbm, dy_ref),
                (u_hbm, u_ref),
                (place_hbm, place_ref),
                (parent_hbm, parent_ref),
            )
        )
    ]
    for fetch in fetches:
        fetch.start()

    for i in range(1, ranks):
        pl.semaphore_signal(
            barrier, inc=1, device_id={"mp": lax.rem(rank + i, ranks)}, device_id_type=MESH
        )
    loop(devices - 1, greet)

    stores = []

    def store(src, dst):
        copy = pltpu.make_async_copy(src, dst, out_sem.at[len(stores)])
        copy.start()
        stores.append(copy)

    first_row = lax.broadcasted_iota(jnp.int32, (T, wide), 0) == 0
    last_row = lax.broadcasted_iota(jnp.int32, (T, wide), 0) == T - 1

    def x_of(i, p):
        return (xp_ref[0, :, lanes(p)] if i == 0 else xr_ref[i - 1, :, lanes(p)]).astype(F32)

    def mix(p, acc):
        f = f_ref[:, lanes(p)]
        parts = []
        for i in range(3):
            x = x_of(i, p)
            prev = jnp.where(first_row, 0.0, pltpu.roll(x, 1, 0))
            m = x + (prev - x) * f
            mixed[i * T : (i + 1) * T, lanes(p)] = m
            parts.append(m)
        return acc + dot3(nn, split(jnp.concatenate(parts, axis=0)), split(down_ref[rows_of(p), :]))

    for fetch in fetches[:4]:
        fetch.wait()
    row_src[...] = xp_ref[0, T - 16 :, :].astype(F32)[15:16]
    partial = loop(steps, mix, jnp.zeros((3 * T, RANK), F32))
    hid_p[...] = partial[:T]
    hid_r[...] = partial[T:]
    for fetch in fetches[4:]:
        fetch.wait()
    pl.semaphore_wait(barrier, devices - 1 + ranks - 1)

    def exchange(src, land, ssem, rsem):
        for i in range(1, ranks):
            peer = lax.rem(rank + i, ranks)
            remote(src, land.at[rank], ssem.at[i], rsem.at[rank], "mp", peer).start()
            pending.append((src, ssem.at[i]))
        land[rank] = src[...]

    def exchanged(land, rsem):
        for i in range(1, ranks):
            source = lax.rem(rank + i, ranks)
            bulk_wait(land.at[source], rsem.at[source])
        total = land[0]
        for i in range(1, ranks):
            total = total + land[i]
        return total

    def send_row(i):
        peer = lax.rem(me + 1 + i, devices)
        remote(row_src, row_land.at[me], row_s, row_r, "dp", peer).start()

    exchange(hid_p, hid_p_land, hid_p_s, hid_p_r)
    loop(devices - 1, send_row)
    pending.append((row_land.at[pl.ds(0, devices - 1)], row_s))
    row_land[me] = row_src[...]
    exchange(hid_r, hid_r_land, hid_r_s, hid_r_r)
    t_sq = lax.broadcasted_iota(jnp.int32, (T, T), 0)
    j_sq = lax.broadcasted_iota(jnp.int32, (T, T), 1)
    before = (j_sq < t_sq).astype(F32).astype(BF16)
    suffix = (j_sq > t_sq).astype(F32).astype(BF16)

    def exact(mask, x):
        hi, mid, low = split3(x)
        return nn(mask, hi) + (nn(mask, mid) + nn(mask, low))

    def decays(lo, hi, p):
        z = dot3(nn, split(th_ref[lo * T : hi * T, :]), split(up_ref[:, lanes(p)]))
        d = -jnp.exp(z + base_ref[:, lanes(p)])
        dec[lo * T : hi * T, lanes(p)] = d
        for i in range(lo, hi):
            at = (i - lo) * T
            e = jnp.exp(exact(suffix if i == 0 else before, d[at : at + T]))
            ef[i * T : (i + 1) * T, lanes(p)] = e
            if i == 0:
                a, b = kv_ref[0, 0, :, lanes(p)], kv_ref[1, 0, :, lanes(p)]
            else:
                a, b = rkv_ref[0, i - 1, :, lanes(p)], dy_ref[i - 1, :, lanes(p)]
            packed = pack_diag(left2(tn, split(a.astype(F32) * e), b))
            for n in range(blocks):
                part = packed[:, n * LANES : (n + 1) * LANES].reshape(dests, per, LANES)
                at = pl.ds((p * blocks + n) * dests, dests)
                if i == 0:
                    send_f1[at] = part
                else:
                    send_b1[at, i - 1] = part

    def route(n, src, dst_of):
        def send(i):
            peer = lax.rem(me + 1 + i, devices)
            remote(src.at[peer], dst_of(me), route_s.at[n], route_r.at[n], "dp", peer).start()

        loop(devices - 1, send)
        pending.append((src.at[pl.ds(0, devices - 1)], route_s.at[n]))

    def column(row):
        n = row.shape[1]
        diagonal = lax.broadcasted_iota(jnp.int32, (n, n), 0) == lax.broadcasted_iota(
            jnp.int32, (n, n), 1
        )
        return jnp.sum(jnp.where(diagonal, row, 0), axis=1, keepdims=True)

    placed, parents = place_ref[...], parent_ref[...]
    pairs_at = (devices, 2 * devices)
    match = column(placed) == parents
    slot = lax.broadcasted_iota(jnp.int32, pairs_at, 0)
    owner_vec[...] = jnp.max(jnp.where(match, slot, 0), axis=0, keepdims=True)
    match = column(parents) == placed
    response = lax.broadcasted_iota(jnp.int32, pairs_at[::-1], 0)
    first_vec[...] = jnp.min(
        jnp.where(match, response, 2 * devices - 1), axis=0, keepdims=True
    )
    last_vec[...] = jnp.max(jnp.where(match, response, 0), axis=0, keepdims=True)
    indices = [
        pltpu.make_async_copy(src, dst, index_sem.at[n])
        for n, (src, dst) in enumerate(
            ((owner_vec, owner_ref), (first_vec, first_ref), (last_vec, last_ref))
        )
    ]
    for copy in indices:
        copy.start()
    for copy in indices:
        copy.wait()

    def gap_mask(shape, t_axis, level):
        t = lax.broadcasted_iota(jnp.int32, shape, t_axis)
        j = lax.broadcasted_iota(jnp.int32, shape, 1 - t_axis)
        b = LEVELS[level]
        second = (t & b) != 0
        late = second & (j >= (t & -b)) & (j < t)
        early = ~second & (j > t) & (j <= (t | (b - 1)))
        return (late | early).astype(F32).astype(BF16)

    for level in range(len(LEVELS)):
        gaps_ref[level * T : (level + 1) * T, :] = gap_mask((T, T), 0, level)
    for level in range(0, len(LEVELS), 2):
        both = [gap_mask((T, T), 1, level + n) for n in range(2)]
        gaps_t_ref[:, level * T : (level + 2) * T] = jnp.concatenate(both, axis=1)
    t_row = lax.broadcasted_iota(jnp.int32, (T, wide), 0)
    s_col = lax.broadcasted_iota(jnp.int32, (T, wide), 1) & (T - 1)
    apart = t_row ^ s_col
    for level, b in enumerate(LEVELS):
        masks_ref[level * T : (level + 1) * T, :] = ((apart >= b) & (apart < 2 * b)).astype(F32)

    th_ref[:T, :] = jnp.tanh(exchanged(hid_p_land, hid_p_r))
    loop(steps, functools.partial(decays, 0, 1))
    bulk_wait(row_land.at[pl.ds(0, devices - 1)], row_r)
    lead_rows = [row_land[owner_ref[0, 2 * me + i]] for i in range(2)]
    row8 = lax.broadcasted_iota(jnp.int32, (8, channels), 0)
    lead[...] = jnp.where(row8 == 0, lead_rows[0], jnp.where(row8 == 1, lead_rows[1], 0.0))

    def lead_mix(p, acc):
        fl = f_ref[:, lanes(p)] * lead[:, lanes(p)]
        for i in range(2):
            at = (i + 1) * T
            mixed[at : at + 1, lanes(p)] = mixed[at : at + 1, lanes(p)] + fl[i : i + 1]
        return acc + dot3(nn, split(fl), split(down_ref[rows_of(p), :]))

    lead_hid[...] = loop(steps, lead_mix, jnp.zeros((8, RANK), F32))
    exchange(lead_hid, lead_land, lead_s, lead_r)
    route(0, send_f1, lambda m: recv_f1.at[m])
    recv_f1[me] = send_f1[me]

    hidden = exchanged(hid_r_land, hid_r_r)
    th_ref[T:, :] = jnp.tanh(hidden)
    extra = exchanged(lead_land, lead_r)
    for i in range(2):
        at = (i + 1) * T
        th_ref[at : at + 1, :] = jnp.tanh(hidden[i * T : i * T + 1] + extra[i : i + 1])
    loop(steps, functools.partial(decays, 1, 3))
    route(1, send_b1, lambda m: recv_b1.at[pl.ds(2 * m, 2)])
    recv_b1[pl.ds(2 * me, 2)] = send_b1[me]

    bulk_wait(recv_f1.at[pl.ds(0, devices - 1)], route_r.at[0])

    def shuffle_f(n):
        send_f2[n, 0] = recv_f1[owner_ref[0, 2 * n]]
        send_f2[n, 1] = recv_f1[owner_ref[0, 2 * n + 1]]

    loop(devices, shuffle_f)
    route(2, send_f2, lambda m: recv_f2.at[m])
    recv_f2[me] = send_f2[me]

    ones_block = (
        (
            lax.broadcasted_iota(jnp.int32, (wide, wide), 0) // HEAD
            == lax.broadcasted_iota(jnp.int32, (wide, wide), 1) // HEAD
        )
        .astype(F32)
        .astype(BF16)
    )
    deep = len(LEVELS) - 1

    def inner(i, p):
        cols = lanes(p)
        rb, kb, vb = (rkv_ref[n, i, :, cols] for n in range(3))
        yb = dy_ref[i, :, cols]
        r, k, v, y = (a.astype(F32) for a in (rb, kb, vb, yb))
        d = dec[(i + 1) * T : (i + 2) * T, cols]
        u = u_ref[:, cols]
        y_diag = block_diag(yb)
        sym = jnp.where(t_row > s_col, nt(yb, block_diag(vb)), nt(vb, y_diag))
        gap = exact(gaps_ref[: deep * T, :], d)
        att = jnp.zeros((T, wide), F32)
        dr = jnp.zeros((T, wide), F32)
        dk = jnp.zeros((T, wide), F32)
        dgaps = []
        for level, b in enumerate(LEVELS):
            second = (t_row & b) != 0
            mask = masks_ref[level * T : (level + 1) * T, :]
            side = jnp.where(second, r, k)
            if level == deep:
                w = side.astype(BF16)
                wd = block_diag(w)
                att = att + mask * nt(w, wd)
                g = left2(nn, split(mask * sym), wd)
            else:
                x = jnp.exp(gap[level * T : (level + 1) * T])
                w = side * x
                ws = split(w)
                wd = tuple(block_diag(a) for a in ws)
                att = att + mask * dot3(nt, ws, wd)
                dw = dot3(nn, split(mask * sym), wd)
                dgaps.append(w * dw)
                g = x * dw
            dr = dr + jnp.where(second, g, 0.0)
            dk = dk + jnp.where(second, 0.0, g)
        dgap = jnp.concatenate(dgaps, axis=0)
        dd_loc[i, :, cols] = right2(nn, gaps_t_ref[:, : deep * T], split(dgap))
        self_a = left2(nn, split(r * u * k), ones_block)
        self_b = left2(nn, split(y * v), ones_block)
        dv = left2(nn, split(jnp.where(s_col > t_row, att, 0.0)), y_diag) + self_a * y
        dr_loc[i, :, cols] = dr + u * k * self_b
        rkv_out[1, i, :, cols] = (dk + u * r * self_b).astype(BF16)
        rkv_out[2, i, :, cols] = dv.astype(BF16)
        part = jnp.sum(r * k * self_b, axis=0, keepdims=True)
        if i == 0:
            vec[1, :, cols] = part
        else:
            vec[1, :, cols] = vec[1, :, cols] + part

    loop(steps, functools.partial(inner, 0))
    bulk_wait(recv_b1.at[pl.ds(0, 2 * (devices - 1))], route_r.at[1])

    def shuffle_b(n):
        send_b2[n] = recv_b1[first_ref[0, n]] + recv_b1[last_ref[0, n]]

    loop(devices, shuffle_b)
    route(3, send_b2, lambda m: recv_b2.at[m])
    recv_b2[me] = send_b2[me]
    loop(steps, functools.partial(inner, 1))

    def landed(ref, p, *i):
        parts = [
            ref[(pl.ds((p * blocks + n) * dests, dests), *i)].reshape(HEAD, LANES)
            for n in range(blocks)
        ]
        return tuple(block_diag(a) for a in split(jnp.concatenate(parts, axis=1)))

    def outer_r(p):
        for i in range(2):
            sd = landed(recv_f2, p, i)
            rows = slice((i + 1) * T, (i + 2) * T)
            r = rkv_ref[0, i, :, lanes(p)].astype(F32)
            drs = ef[rows, lanes(p)] * right2(nt, dy_ref[i, :, lanes(p)], sd)
            rkv_out[0, i, :, lanes(p)] = (dr_loc[i, :, lanes(p)] + drs).astype(BF16)
            dd = right2(nn, suffix, split(r * drs)) + dd_loc[i, :, lanes(p)]
            dz_ref[rows, lanes(p)] = dd * dec[rows, lanes(p)]

    def outer_p(p):
        sd = landed(recv_b2, p)
        e = ef[:T, lanes(p)]
        k = kv_ref[0, 0, :, lanes(p)].astype(F32)
        dk = e * right2(nt, kv_ref[1, 0, :, lanes(p)], sd)
        dv = dot3(nn, split(k * e), sd)
        kv_out[0, 0, :, lanes(p)] = dk.astype(BF16)
        kv_out[1, 0, :, lanes(p)] = dv.astype(BF16)
        dd = right2(nn, before, split(k * dk))
        dz_ref[:T, lanes(p)] = dd * dec[:T, lanes(p)]

    def dth_part(lo, hi, p, acc):
        return acc + dot3(nt, split(dz_ref[lo * T : hi * T, lanes(p)]), split(up_ref[:, lanes(p)]))

    bulk_wait(recv_f2.at[pl.ds(0, devices - 1)], route_r.at[2])
    loop(steps, outer_r)
    dth_r_src[...] = loop(
        steps, functools.partial(dth_part, 1, 3), jnp.zeros((2 * T, RANK), F32)
    )
    exchange(dth_r_src, dth_r_land, dth_r_s, dth_r_r)
    bulk_wait(recv_b2.at[pl.ds(0, devices - 1)], route_r.at[3])
    loop(steps, outer_p)
    dth_p_src[...] = loop(steps, functools.partial(dth_part, 0, 1), jnp.zeros((T, RANK), F32))
    exchange(dth_p_src, dth_p_land, dth_p_s, dth_p_r)
    store(rkv_out, rkv_hbm_out)
    store(kv_out, kv_hbm_out)

    place = [lax.rem(me // g, n) for g, n in stages]
    size = [channels // 2]
    for g, n in stages:
        size.append(size[-1] // n)
    lands = (land0, land1, land2)
    sums = (cur1, cur2, cur3)

    def peers(stage):
        g, n = stages[stage]
        q = place[stage]
        for i in range(1, n):
            other = lax.rem(q + i, n)
            yield i, other, me + (other - q) * g

    def addend(stream, stage, q):
        rows = size[stage + 1]
        ref, base = (grad, stream * size[0]) if stage == 0 else (sums[stage - 1].at[stream], 0)
        return ref.at[pl.ds(pl.multiple_of(base + q * rows, 8), rows)]

    def rs_start(stream, stage):
        for i, other, peer in peers(stage):
            part = addend(stream, stage, other)
            ssem, rsem = rs_s.at[stream, stage, i], rs_r.at[stream, stage, place[stage]]
            remote(part, lands[stage].at[stream, place[stage]], ssem, rsem, "dp", peer).start()
            pending.append((part, ssem))

    def rs_finish(stream, stage):
        total = addend(stream, stage, place[stage])[...]
        for i, other, peer in peers(stage):
            bulk_wait(lands[stage].at[stream, other], rs_r.at[stream, stage, other])
            total = total + lands[stage][stream, other]
        sums[stage][stream] = total

    offs = [0]
    for stage in range(3):
        offs.append(offs[-1] + place[stage] * size[stage + 1])

    def piece(stream, stage, q):
        rows = size[stage + 1]
        at = stream * size[0] + offs[stage] + q * rows
        return fin.at[pl.ds(pl.multiple_of(at, 8), rows)]

    def ag_start(stream, stage):
        q = place[stage]
        mine = piece(stream, stage, q)
        if stage == 2:
            mine[...] = sums[2][stream]
        for i, other, peer in peers(stage):
            ssem, rsem = ag_s.at[stream, stage, i], ag_r.at[stream, stage, q]
            remote(mine, mine, ssem, rsem, "dp", peer).start()
            pending.append((mine, ssem))

    def ag_finish(stream, stage):
        for i, other, peer in peers(stage):
            bulk_wait(piece(stream, stage, other), ag_r.at[stream, stage, other])

    def advance(stream, step):
        if step < 3:
            rs_finish(stream, step)
        else:
            ag_finish(stream, 5 - step)
        if step < 2:
            rs_start(stream, step + 1)
        elif step < 5:
            ag_start(stream, 4 - step)
        else:
            rows = pl.ds(stream * size[0], size[0])
            store(fin.at[rows], grad_hbm_out.at[rows])

    def vec_start(stage):
        q = place[stage]
        at = sum(m for _, m in stages[:stage])
        mine = vec.at[pl.ds(3 * stage, 3)]
        for i, other, peer in peers(stage):
            ssem, rsem = vec_s.at[stage, i], vec_r.at[stage, q]
            remote(mine, vec_land.at[at + q], ssem, rsem, "dp", peer).start()
            pending.append((mine, ssem))
        vec_land[at + q] = vec[3 * stage : 3 * stage + 3]

    def vec_finish(stage):
        at = sum(m for _, m in stages[:stage])
        for i, other, peer in peers(stage):
            bulk_wait(vec_land.at[at + other], vec_r.at[stage, other])
        total = vec_land[at]
        for i in range(1, stages[stage][1]):
            total = total + vec_land[at + i]
        if stage == 2:
            vec_out[...] = total
        else:
            vec[3 * stage + 3 : 3 * stage + 6] = total

    def dh_piece(stage, q):
        g = stages[stage][0]
        return dh_land.at[pl.ds(2 * (me - lax.rem(me, g) + (q - place[stage]) * g), 2 * g)]

    def dh_start(stage):
        q = place[stage]
        mine = dh_piece(stage, q)
        for i, other, peer in peers(stage):
            remote(mine, mine, dh_s.at[stage, i], dh_r.at[stage, q], "dp", peer).start()
            pending.append((mine, dh_s.at[stage, i]))

    def dh_finish(stage):
        for i, other, peer in peers(stage):
            bulk_wait(dh_piece(stage, other), dh_r.at[stage, other])

    def up_grads(p):
        dz = dz_ref[:, lanes(p)]
        g = dot3(tn, split(th_ref[...]), split(dz))
        for n in range(blocks):
            rows = pl.ds(pl.multiple_of(p * wide + n * LANES, LANES), LANES)
            grad[rows, :] = g[:, n * LANES : (n + 1) * LANES]
        vec[0, :, lanes(p)] = jnp.sum(dz, axis=0, keepdims=True)

    def down_grads(p):
        rows = pl.ds(pl.multiple_of(channels + p * wide, LANES), wide)
        grad[rows, :] = dot3(tn, split(mixed[:, lanes(p)]), split(dh_ref[...]))

    def both_streams(stream, fn):
        half = (steps + 1) // 2
        loop(half, fn)
        rs_start(stream, 0)
        loop(steps - half, lambda p: fn(p + half))
        rs_start(stream + 1, 0)

    both_streams(0, up_grads)

    th = th_ref[T:, :]
    dh_ref[T:, :] = exchanged(dth_r_land, dth_r_r) * (1.0 - th * th)
    for i in range(2):
        dh_land[2 * me + i] = dh_ref[(i + 1) * T : (i + 1) * T + 1, :]
    dh_start(0)
    advance(0, 0)
    advance(1, 0)
    th = th_ref[:T, :]
    dh_ref[:T, :] = exchanged(dth_p_land, dth_p_r) * (1.0 - th * th)
    both_streams(2, down_grads)

    def x_grads(p):
        f = f_ref[:, lanes(p)]
        dm = dot3(nt, split(dh_ref[...]), split(down_ref[rows_of(p), :]))
        mix_sum = jnp.zeros((1, wide), F32)
        for i in range(3):
            x = x_of(i, p)
            g = dm[i * T : (i + 1) * T]
            ahead = jnp.where(last_row, 0.0, pltpu.roll(g, T - 1, 0))
            first = 0.0 if i == 0 else lead[i - 1 : i, lanes(p)]
            prev = jnp.where(first_row, first, pltpu.roll(x, 1, 0))
            dx = g + (ahead - g) * f
            mix_sum = mix_sum + jnp.sum(g * (prev - x), axis=0, keepdims=True)
            if i == 0:
                xp_out[0, :, lanes(p)] = dx.astype(BF16)
                xp_tail[:, lanes(p)] = dx[T - 16 :]
            else:
                xr_out[i - 1, :, lanes(p)] = dx.astype(BF16)
        vec[2, :, lanes(p)] = mix_sum

    def x_tail(late, p):
        f = f_ref[:, lanes(p)]
        more = f * dot3(nt, split(late), split(down_ref[rows_of(p), :]))[0:1]
        tail = xp_tail[:, lanes(p)]
        at_end = lax.broadcasted_iota(jnp.int32, (16, wide), 0) == 15
        xp_out[0, T - 16 :, lanes(p)] = jnp.where(at_end, tail + more, tail).astype(BF16)

    for stream, step in ((2, 0), (0, 1), (3, 0), (1, 1)):
        advance(stream, step)
    dh_finish(0)
    dh_start(1)
    loop(steps, x_grads)
    vec_start(0)
    store(xr_out, xr_hbm_out)
    for stream, step in ((2, 1), (0, 2), (3, 1), (1, 2)):
        advance(stream, step)
    dh_finish(1)
    dh_start(2)
    vec_finish(0)
    vec_start(1)
    for stream, step in ((2, 2), (0, 3), (3, 2), (1, 3)):
        advance(stream, step)
    vec_finish(1)
    vec_start(2)
    dh_finish(2)
    late = dh_land[first_ref[0, me]] + dh_land[last_ref[0, me]]
    loop(steps, functools.partial(x_tail, jnp.broadcast_to(late, (8, RANK))))
    store(xp_out, xp_hbm_out)
    for stream, step in ((2, 3), (0, 4), (3, 3), (1, 4)):
        advance(stream, step)
    vec_finish(2)
    store(vec_out, vec_hbm_out)
    for stream, step in ((2, 4), (0, 5), (3, 4), (1, 5), (2, 5), (3, 5)):
        advance(stream, step)

    for view, sem in pending:
        bulk_wait(view, sem)
    for copy in stores:
        copy.wait()


def results(pairs, *refs):
    sources, outs, held, (in_sem, out_sem) = refs[:6], refs[6:15], refs[15:21], refs[21:]
    loads = [
        pltpu.make_async_copy(a, b, in_sem.at[n]) for n, (a, b) in enumerate(zip(sources, held))
    ]
    for load in loads:
        load.start()
    moves = [[(held[n], outs[n])] for n in range(4)]
    moves.append([(held[4].at[pl.ds(pairs * LANES, pairs * LANES)], outs[4])])
    for p in range(pairs):
        lanes = pl.ds(p * LANES, LANES)
        moves[4].append((held[4].at[lanes], outs[5].at[:, lanes]))
    moves.append([(held[5].at[n], outs[6 + n]) for n in range(3)])
    copies = []
    for load, group in zip(loads, moves):
        load.wait()
        for src, dst in group:
            copies.append(pltpu.make_async_copy(src, dst, out_sem.at[len(copies)]))
            copies[-1].start()
    for copy in copies:
        copy.wait()


def per_device(
    query_text_memory,
    query_text_feed,
    reply_acceptor_memory,
    reply_feed,
    reply_cotangent_vector,
    query_placement,
    reply_parent_query,
    fading_narrowing,
    fading_widening,
    fading_anchor_rate,
    self_emphasis,
    lagged_token_fraction,
):
    devices = lax.axis_size("dp")
    ranks = lax.axis_size("mp")
    channels = query_text_feed.shape[2]
    pairs = channels // LANES
    per = HEAD * pairs // devices
    stages = stages_of(devices)
    size = [channels // 2]
    for g, n in stages:
        size.append(size[-1] // n)

    def vmem(*shape, dtype=F32):
        return pltpu.VMEM(shape, dtype)

    operands = (
        query_placement[None],
        reply_parent_query[None],
        query_text_memory,
        query_text_feed,
        reply_acceptor_memory,
        reply_feed,
        reply_cotangent_vector,
        fading_narrowing,
        fading_widening,
        fading_anchor_rate[None],
        self_emphasis[None],
        lagged_token_fraction[None],
    )
    dma = pltpu.SemaphoreType.DMA
    shapes = [
        jax.ShapeDtypeStruct(a.shape, BF16)
        for a in (reply_acceptor_memory, reply_feed, query_text_memory, query_text_feed)
    ]
    scratch = [pltpu.VMEM(a.shape, a.dtype) for a in shapes]
    scratch += [vmem(3, 1, channels)]
    scratch += [pltpu.VMEM(a.shape, a.dtype) for a in operands]
    scratch += [
        vmem(1, 2 * devices, dtype=jnp.int32),
        vmem(1, devices, dtype=jnp.int32),
        vmem(1, devices, dtype=jnp.int32),
        pltpu.SMEM((1, 2 * devices), jnp.int32),
        pltpu.SMEM((1, devices), jnp.int32),
        pltpu.SMEM((1, devices), jnp.int32),
        vmem(len(LEVELS) * T, T, dtype=BF16),
        vmem(T, len(LEVELS) * T, dtype=BF16),
        vmem(len(LEVELS) * T, min(2 * LANES, channels)),
        vmem(1, channels),
        vmem(devices, 1, channels),
        vmem(3 * T, channels),
        vmem(T, RANK),
        vmem(ranks, T, RANK),
        vmem(2 * T, RANK),
        vmem(ranks, 2 * T, RANK),
        vmem(8, channels),
        vmem(8, RANK),
        vmem(ranks, 8, RANK),
        vmem(3 * T, channels),
        vmem(3 * T, channels),
        vmem(devices, per, LANES),
        vmem(devices, per, LANES),
        vmem(devices, 2, per, LANES),
        vmem(2 * devices, per, LANES),
        vmem(devices, 2, per, LANES),
        vmem(devices, 2, per, LANES),
        vmem(devices, per, LANES),
        vmem(devices, per, LANES),
        vmem(2, T, channels),
        vmem(2, T, channels),
        vmem(3 * T, RANK),
        vmem(3 * T, channels),
        vmem(2 * T, RANK),
        vmem(ranks, 2 * T, RANK),
        vmem(T, RANK),
        vmem(ranks, T, RANK),
        vmem(3 * T, RANK),
        vmem(2 * devices, 1, RANK),
        vmem(16, channels),
        vmem(9, 1, channels),
        vmem(sum(n for _, n in stages), 3, 1, channels),
        vmem(2 * channels, RANK),
        vmem(4, size[1], RANK),
        vmem(4, size[2], RANK),
        vmem(4, size[3], RANK),
        vmem(4, stages[0][1], size[1], RANK),
        vmem(4, stages[1][1], size[2], RANK),
        vmem(4, stages[2][1], size[3], RANK),
        vmem(2 * channels, RANK),
        dma((len(operands),)),
        dma((3,)),
        dma((9,)),
        dma,
        dma,
        dma((ranks,)),
        dma((ranks,)),
        dma((ranks,)),
        dma((ranks,)),
        dma((ranks,)),
        dma((ranks,)),
        dma((4,)),
        dma((4,)),
        dma((ranks,)),
        dma((ranks,)),
        dma((ranks,)),
        dma((ranks,)),
        dma((3, 8)),
        dma((3, 8)),
        dma((3, 8)),
        dma((3, 8)),
        dma((4, 3, 8)),
        dma((4, 3, 8)),
        dma((4, 3, 8)),
        dma((4, 3, 8)),
    ]
    far = pl.BlockSpec(memory_space=pltpu.HBM)
    moved = pl.pallas_call(
        functools.partial(body, devices, ranks, channels),
        out_shape=(
            *shapes,
            jax.ShapeDtypeStruct((2 * channels, RANK), F32),
            jax.ShapeDtypeStruct((3, 1, channels), F32),
        ),
        in_specs=[far] * len(operands),
        out_specs=[far] * 6,
        scratch_shapes=scratch,
        compiler_params=pltpu.CompilerParams(
            collective_id=0, has_side_effects=True, vmem_limit_bytes=VMEM
        ),
    )(*operands)
    rkv, xr, kv, xp, down, up, *vectors = pl.pallas_call(
        functools.partial(results, pairs),
        out_shape=(
            *shapes,
            jax.ShapeDtypeStruct(fading_narrowing.shape, F32),
            jax.ShapeDtypeStruct(fading_widening.shape, F32),
            *[jax.ShapeDtypeStruct((1, channels), F32)] * 3,
        ),
        in_specs=[far] * 6,
        out_specs=[far] * 9,
        scratch_shapes=[pltpu.VMEM(a.shape, a.dtype) for a in moved]
        + [dma((6,)), dma((8 + pairs,))],
        compiler_params=pltpu.CompilerParams(vmem_limit_bytes=VMEM),
    )(*moved)
    return rkv, xr, kv, xp, down, up, *[v.reshape(channels) for v in vectors]


def solution(mesh):
    in_specs = (
        P(None, "dp", None, "mp"),
        P("dp", None, "mp"),
        P(None, "dp", None, "mp"),
        P("dp", None, "mp"),
        P("dp", None, "mp"),
        P(),
        P(),
        P("mp", None),
        P(None, "mp"),
        P("mp"),
        P("mp"),
        P("mp"),
    )
    out_specs = (
        P(None, "dp", None, "mp"),
        P("dp", None, "mp"),
        P(None, "dp", None, "mp"),
        P("dp", None, "mp"),
        P("mp", None),
        P(None, "mp"),
        P("mp"),
        P("mp"),
        P("mp"),
    )
    return jax.shard_map(
        per_device, mesh=mesh, in_specs=in_specs, out_specs=out_specs, check_vma=False
    )
```

```python
import functools

import jax
import jax.numpy as jnp
from jax import lax
from jax.experimental import pallas as pl
from jax.experimental.pallas import tpu as pltpu
from jax.sharding import PartitionSpec as P

HEAD = 64
T = 64
LANES = 128
RANK = 128
VMEM = 63 * 1024 * 1024
LEVELS = (32, 16, 8, 4, 2, 1)
MESH = pl.DeviceIdType.MESH
F32 = jnp.float32
BF16 = jnp.bfloat16


def stages_of(devices):
    if devices == 64:
        return ((1, 2), (2, 4), (8, 8))
    return ((1, 2), (2, 2), (4, devices // 4))


def nn(a, b):
    return lax.dot_general(a, b, (((1,), (0,)), ((), ())), preferred_element_type=F32)


def nt(a, b):
    return lax.dot_general(a, b, (((1,), (1,)), ((), ())), preferred_element_type=F32)


def tn(a, b):
    return lax.dot_general(a, b, (((0,), (0,)), ((), ())), preferred_element_type=F32)


def split(x):
    hi = x.astype(BF16)
    return hi, (x - hi.astype(F32)).astype(BF16)


def split3(x):
    hi = x.astype(BF16)
    rest = x - hi.astype(F32)
    mid = rest.astype(BF16)
    return hi, mid, (rest - mid.astype(F32)).astype(BF16)


def dot3(dot, a, b):
    return dot(a[0], b[0]) + (dot(a[0], b[1]) + dot(a[1], b[0]))


def left2(dot, a, b):
    return dot(a[0], b) + dot(a[1], b)


def right2(dot, a, b):
    return dot(a, b[0]) + dot(a, b[1])


def block_diag(x):
    head = lax.broadcasted_iota(jnp.int32, x.shape, 1) // HEAD
    zero = jnp.zeros_like(x)
    return jnp.concatenate(
        [jnp.where(head == h, x, zero) for h in range(x.shape[1] // HEAD)], axis=0
    )


def pack_diag(m):
    n = m.shape[1] // HEAD
    head = lax.broadcasted_iota(jnp.int32, (HEAD, m.shape[1]), 1) // HEAD
    out = m[:HEAD]
    for h in range(1, n):
        out = jnp.where(head == h, m[h * HEAD : (h + 1) * HEAD], out)
    return out


def body(
    devices,
    ranks,
    channels,
    place_hbm,
    parent_hbm,
    kv_hbm,
    xp_hbm,
    rkv_hbm,
    xr_hbm,
    dy_hbm,
    down_hbm,
    up_hbm,
    base_hbm,
    u_hbm,
    f_hbm,
    rkv_hbm_out,
    xr_hbm_out,
    kv_hbm_out,
    xp_hbm_out,
    grad_hbm_out,
    vec_hbm_out,
    rkv_out,
    xr_out,
    kv_out,
    xp_out,
    vec_out,
    place_ref,
    parent_ref,
    kv_ref,
    xp_ref,
    rkv_ref,
    xr_ref,
    dy_ref,
    down_ref,
    up_ref,
    base_ref,
    u_ref,
    f_ref,
    owner_vec,
    first_vec,
    last_vec,
    owner_ref,
    first_ref,
    last_ref,
    gaps_ref,
    gaps_t_ref,
    masks_ref,
    row_src,
    row_land,
    mixed,
    hid_p,
    hid_p_land,
    hid_r,
    hid_r_land,
    lead,
    lead_hid,
    lead_land,
    dec,
    ef,
    send_f1,
    recv_f1,
    send_b1,
    recv_b1,
    send_f2,
    recv_f2,
    send_b2,
    recv_b2,
    dr_loc,
    dd_loc,
    th_ref,
    dz_ref,
    dth_r_src,
    dth_r_land,
    dth_p_src,
    dth_p_land,
    dh_ref,
    dh_land,
    xp_tail,
    vec,
    vec_land,
    grad,
    cur1,
    cur2,
    cur3,
    land0,
    land1,
    land2,
    fin,
    in_sem,
    index_sem,
    out_sem,
    row_s,
    row_r,
    hid_p_s,
    hid_p_r,
    hid_r_s,
    hid_r_r,
    lead_s,
    lead_r,
    route_s,
    route_r,
    dth_r_s,
    dth_r_r,
    dth_p_s,
    dth_p_r,
    dh_s,
    dh_r,
    vec_s,
    vec_r,
    rs_s,
    rs_r,
    ag_s,
    ag_r,
):
    me = lax.axis_index("dp")
    rank = lax.axis_index("mp")
    wide = min(2 * LANES, channels)
    blocks = wide // LANES
    steps = channels // wide
    per = HEAD * (channels // LANES) // devices
    dests = HEAD // per
    stages = stages_of(devices)

    def lanes(p):
        if isinstance(p, int):
            return pl.ds(p * wide, wide)
        return pl.ds(pl.multiple_of(p * wide, LANES), wide)

    rows_of = lanes

    def loop(n, fn, init=None):
        if init is None:
            lax.fori_loop(0, n, lambda i, c: (fn(i), c)[1], 0)
            return None
        return lax.fori_loop(0, n, fn, init)

    def unrolled(n, fn, init=None):
        for i in range(n):
            init = fn(i) if init is None else fn(i, init)
        return init

    def by_two(n, fn):
        if n % 2:
            return loop(n, fn)
        return loop(n // 2, lambda i: (fn(2 * i), fn(2 * i + 1)))

    def remote(src, dst, ssem, rsem, axis, peer):
        return pltpu.make_async_remote_copy(
            src_ref=src,
            dst_ref=dst,
            send_sem=ssem,
            recv_sem=rsem,
            device_id={axis: peer},
            device_id_type=MESH,
        )

    def bulk_wait(view, sem):
        pltpu.make_async_copy(view, view, sem).wait()

    pending = []
    settled = [0]

    def settle():
        for view, sem in pending[: settled[0]]:
            bulk_wait(view, sem)
        del pending[: settled[0]]
        settled[0] = len(pending)

    barrier = pltpu.get_barrier_semaphore()

    def greet(i):
        pl.semaphore_signal(
            barrier, inc=1, device_id={"dp": lax.rem(me + 1 + i, devices)}, device_id_type=MESH
        )

    fetches = [
        pltpu.make_async_copy(src, dst, in_sem.at[n])
        for n, (src, dst) in enumerate(
            (
                (xp_hbm, xp_ref),
                (xr_hbm, xr_ref),
                (f_hbm, f_ref),
                (down_hbm, down_ref),
                (up_hbm, up_ref),
                (base_hbm, base_ref),
                (kv_hbm, kv_ref),
                (rkv_hbm, rkv_ref),
                (dy_hbm, dy_ref),
                (u_hbm, u_ref),
                (place_hbm, place_ref),
                (parent_hbm, parent_ref),
            )
        )
    ]
    for fetch in fetches:
        fetch.start()

    for i in range(1, ranks):
        pl.semaphore_signal(
            barrier, inc=1, device_id={"mp": lax.rem(rank + i, ranks)}, device_id_type=MESH
        )
    loop(devices - 1, greet)

    stores = []

    def store(src, dst):
        copy = pltpu.make_async_copy(src, dst, out_sem.at[len(stores)])
        copy.start()
        stores.append(copy)

    first_row = lax.broadcasted_iota(jnp.int32, (T, wide), 0) == 0
    last_row = lax.broadcasted_iota(jnp.int32, (T, wide), 0) == T - 1

    def x_of(i, p):
        return (xp_ref[0, :, lanes(p)] if i == 0 else xr_ref[i - 1, :, lanes(p)]).astype(F32)

    def mix(p, acc):
        f = f_ref[:, lanes(p)]
        parts = []
        for i in range(3):
            x = x_of(i, p)
            prev = jnp.where(first_row, 0.0, pltpu.roll(x, 1, 0))
            m = x + (prev - x) * f
            mixed[i * T : (i + 1) * T, lanes(p)] = m
            parts.append(m)
        return acc + dot3(nn, split(jnp.concatenate(parts, axis=0)), split(down_ref[rows_of(p), :]))

    for fetch in fetches[:4]:
        fetch.wait()
    row_src[...] = xp_ref[0, T - 16 :, :].astype(F32)[15:16]
    partial = unrolled(steps, mix, jnp.zeros((3 * T, RANK), F32))
    hid_p[...] = partial[:T]
    hid_r[...] = partial[T:]
    for fetch in fetches[4:]:
        fetch.wait()
    def column(row):
        n = row.shape[1]
        diagonal = lax.broadcasted_iota(jnp.int32, (n, n), 0) == lax.broadcasted_iota(
            jnp.int32, (n, n), 1
        )
        return jnp.sum(jnp.where(diagonal, row, 0), axis=1, keepdims=True)

    placed, parents = place_ref[...], parent_ref[...]
    pairs_at = (devices, 2 * devices)
    match = column(placed) == parents
    slot = lax.broadcasted_iota(jnp.int32, pairs_at, 0)
    owner_vec[...] = jnp.max(jnp.where(match, slot, 0), axis=0, keepdims=True)
    match = column(parents) == placed
    response = lax.broadcasted_iota(jnp.int32, pairs_at[::-1], 0)
    first_vec[...] = jnp.min(
        jnp.where(match, response, 2 * devices - 1), axis=0, keepdims=True
    )
    last_vec[...] = jnp.max(jnp.where(match, response, 0), axis=0, keepdims=True)
    indices = [
        pltpu.make_async_copy(src, dst, index_sem.at[n])
        for n, (src, dst) in enumerate(
            ((owner_vec, owner_ref), (first_vec, first_ref), (last_vec, last_ref))
        )
    ]
    for copy in indices:
        copy.start()
    pl.semaphore_wait(barrier, devices - 1 + ranks - 1)

    def exchange(src, land, ssem, rsem):
        for i in range(1, ranks):
            peer = lax.rem(rank + i, ranks)
            remote(src, land.at[rank], ssem.at[i], rsem.at[rank], "mp", peer).start()
            pending.append((src, ssem.at[i]))
        land[rank] = src[...]

    def exchanged(land, rsem):
        for i in range(1, ranks):
            source = lax.rem(rank + i, ranks)
            bulk_wait(land.at[source], rsem.at[source])
        total = land[0]
        for i in range(1, ranks):
            total = total + land[i]
        return total

    def send_row(i):
        peer = lax.rem(me + 1 + i, devices)
        remote(row_src, row_land.at[me], row_s, row_r, "dp", peer).start()

    exchange(hid_p, hid_p_land, hid_p_s, hid_p_r)
    exchange(hid_r, hid_r_land, hid_r_s, hid_r_r)
    loop(devices - 1, send_row)
    pending.append((row_land.at[pl.ds(0, devices - 1)], row_s))
    row_land[me] = row_src[...]
    t_sq = lax.broadcasted_iota(jnp.int32, (T, T), 0)
    j_sq = lax.broadcasted_iota(jnp.int32, (T, T), 1)
    before = (j_sq < t_sq).astype(F32).astype(BF16)
    suffix = (j_sq > t_sq).astype(F32).astype(BF16)

    def exact(mask, x):
        hi, mid, low = split3(x)
        return nn(mask, hi) + (nn(mask, mid) + nn(mask, low))

    def decays(lo, hi, p):
        z = dot3(nn, split(th_ref[lo * T : hi * T, :]), split(up_ref[:, lanes(p)]))
        d = -jnp.exp(z + base_ref[:, lanes(p)])
        dec[lo * T : hi * T, lanes(p)] = d
        for i in range(lo, hi):
            at = (i - lo) * T
            e = jnp.exp(exact(suffix if i == 0 else before, d[at : at + T]))
            ef[i * T : (i + 1) * T, lanes(p)] = e
            if i == 0:
                a, b = kv_ref[0, 0, :, lanes(p)], kv_ref[1, 0, :, lanes(p)]
            else:
                a, b = rkv_ref[0, i - 1, :, lanes(p)], dy_ref[i - 1, :, lanes(p)]
            packed = pack_diag(left2(tn, split(a.astype(F32) * e), b))
            for n in range(blocks):
                part = packed[:, n * LANES : (n + 1) * LANES].reshape(dests, per, LANES)
                at = pl.ds((p * blocks + n) * dests, dests)
                if i == 0:
                    send_f1[at] = part
                else:
                    send_b1[at, i - 1] = part

    def route(n, src, dst_of):
        def send(i):
            peer = lax.rem(me + 1 + i, devices)
            remote(src.at[peer], dst_of(me), route_s.at[n], route_r.at[n], "dp", peer).start()

        loop(devices - 1, send)
        pending.append((src.at[pl.ds(0, devices - 1)], route_s.at[n]))

    th_ref[:T, :] = jnp.tanh(exchanged(hid_p_land, hid_p_r))
    unrolled(steps, functools.partial(decays, 0, 1))
    route(0, send_f1, lambda m: recv_f1.at[m])
    recv_f1[me] = send_f1[me]

    bulk_wait(row_land.at[pl.ds(0, devices - 1)], row_r)
    for copy in indices:
        copy.wait()
    lead_rows = [row_land[owner_ref[0, 2 * me + i]] for i in range(2)]
    row8 = lax.broadcasted_iota(jnp.int32, (8, channels), 0)
    lead[...] = jnp.where(row8 == 0, lead_rows[0], jnp.where(row8 == 1, lead_rows[1], 0.0))

    def lead_mix(p, acc):
        fl = f_ref[:, lanes(p)] * lead[:, lanes(p)]
        for i in range(2):
            at = (i + 1) * T
            mixed[at : at + 1, lanes(p)] = mixed[at : at + 1, lanes(p)] + fl[i : i + 1]
        return acc + dot3(nn, split(fl), split(down_ref[rows_of(p), :]))

    lead_hid[...] = unrolled(steps, lead_mix, jnp.zeros((8, RANK), F32))
    exchange(lead_hid, lead_land, lead_s, lead_r)
    hidden = exchanged(hid_r_land, hid_r_r)
    th_ref[T:, :] = jnp.tanh(hidden)
    extra = exchanged(lead_land, lead_r)
    for i in range(2):
        at = (i + 1) * T
        th_ref[at : at + 1, :] = jnp.tanh(hidden[i * T : i * T + 1] + extra[i : i + 1])
    unrolled(steps, functools.partial(decays, 1, 3))
    route(1, send_b1, lambda m: recv_b1.at[pl.ds(2 * m, 2)])
    recv_b1[pl.ds(2 * me, 2)] = send_b1[me]

    bulk_wait(recv_f1.at[pl.ds(0, devices - 1)], route_r.at[0])

    def shuffle_f(n):
        send_f2[n, 0] = recv_f1[owner_ref[0, 2 * n]]
        send_f2[n, 1] = recv_f1[owner_ref[0, 2 * n + 1]]

    loop(devices, shuffle_f)
    route(2, send_f2, lambda m: recv_f2.at[m])
    recv_f2[me] = send_f2[me]

    def gap_mask(shape, t_axis, level):
        t = lax.broadcasted_iota(jnp.int32, shape, t_axis)
        j = lax.broadcasted_iota(jnp.int32, shape, 1 - t_axis)
        b = LEVELS[level]
        second = (t & b) != 0
        late = second & (j >= (t & -b)) & (j < t)
        early = ~second & (j > t) & (j <= (t | (b - 1)))
        return (late | early).astype(F32).astype(BF16)

    for level in range(len(LEVELS)):
        gaps_ref[level * T : (level + 1) * T, :] = gap_mask((T, T), 0, level)
    for level in range(0, len(LEVELS), 2):
        both = [gap_mask((T, T), 1, level + n) for n in range(2)]
        gaps_t_ref[:, level * T : (level + 2) * T] = jnp.concatenate(both, axis=1)
    t_row = lax.broadcasted_iota(jnp.int32, (T, wide), 0)
    s_col = lax.broadcasted_iota(jnp.int32, (T, wide), 1) & (T - 1)
    apart = t_row ^ s_col
    for level, b in enumerate(LEVELS):
        masks_ref[level * T : (level + 1) * T, :] = ((apart >= b) & (apart < 2 * b)).astype(F32)

    ones_block = (
        (
            lax.broadcasted_iota(jnp.int32, (wide, wide), 0) // HEAD
            == lax.broadcasted_iota(jnp.int32, (wide, wide), 1) // HEAD
        )
        .astype(F32)
        .astype(BF16)
    )
    deep = len(LEVELS) - 1

    def inner(i, p):
        cols = lanes(p)
        rb, kb, vb = (rkv_ref[n, i, :, cols] for n in range(3))
        yb = dy_ref[i, :, cols]
        r, k, v, y = (a.astype(F32) for a in (rb, kb, vb, yb))
        d = dec[(i + 1) * T : (i + 2) * T, cols]
        u = u_ref[:, cols]
        y_diag = block_diag(yb)
        sym = jnp.where(t_row > s_col, nt(yb, block_diag(vb)), nt(vb, y_diag))
        gap = exact(gaps_ref[: deep * T, :], d)
        att = jnp.zeros((T, wide), F32)
        dr = jnp.zeros((T, wide), F32)
        dk = jnp.zeros((T, wide), F32)
        dgaps = []
        for level, b in enumerate(LEVELS):
            second = (t_row & b) != 0
            mask = masks_ref[level * T : (level + 1) * T, :]
            side = jnp.where(second, r, k)
            if level == deep:
                w = side.astype(BF16)
                wd = block_diag(w)
                att = att + mask * nt(w, wd)
                g = left2(nn, split(mask * sym), wd)
            else:
                x = jnp.exp(gap[level * T : (level + 1) * T])
                w = side * x
                ws = split(w)
                wd = tuple(block_diag(a) for a in ws)
                att = att + mask * dot3(nt, ws, wd)
                dw = dot3(nn, split(mask * sym), wd)
                dgaps.append(w * dw)
                g = x * dw
            dr = dr + jnp.where(second, g, 0.0)
            dk = dk + jnp.where(second, 0.0, g)
        dgap = jnp.concatenate(dgaps, axis=0)
        dd_loc[i, :, cols] = right2(nn, gaps_t_ref[:, : deep * T], split(dgap))
        self_a = left2(nn, split(r * u * k), ones_block)
        self_b = left2(nn, split(y * v), ones_block)
        dv = left2(nn, split(jnp.where(s_col > t_row, att, 0.0)), y_diag) + self_a * y
        dr_loc[i, :, cols] = dr + u * k * self_b
        rkv_out[1, i, :, cols] = (dk + u * r * self_b).astype(BF16)
        rkv_out[2, i, :, cols] = dv.astype(BF16)
        part = jnp.sum(r * k * self_b, axis=0, keepdims=True)
        if i == 0:
            vec[1, :, cols] = part
        else:
            vec[1, :, cols] = vec[1, :, cols] + part

    by_two(steps, functools.partial(inner, 0))
    bulk_wait(recv_b1.at[pl.ds(0, 2 * (devices - 1))], route_r.at[1])

    def shuffle_b(n):
        send_b2[n] = recv_b1[first_ref[0, n]] + recv_b1[last_ref[0, n]]

    loop(devices, shuffle_b)
    route(3, send_b2, lambda m: recv_b2.at[m])
    recv_b2[me] = send_b2[me]
    by_two(steps, functools.partial(inner, 1))

    def landed(ref, p, *i):
        parts = [
            ref[(pl.ds((p * blocks + n) * dests, dests), *i)].reshape(HEAD, LANES)
            for n in range(blocks)
        ]
        return tuple(block_diag(a) for a in split(jnp.concatenate(parts, axis=1)))

    def outer_r(p):
        for i in range(2):
            sd = landed(recv_f2, p, i)
            rows = slice((i + 1) * T, (i + 2) * T)
            r = rkv_ref[0, i, :, lanes(p)].astype(F32)
            drs = ef[rows, lanes(p)] * right2(nt, dy_ref[i, :, lanes(p)], sd)
            rkv_out[0, i, :, lanes(p)] = (dr_loc[i, :, lanes(p)] + drs).astype(BF16)
            dd = right2(nn, suffix, split(r * drs)) + dd_loc[i, :, lanes(p)]
            dz_ref[rows, lanes(p)] = dd * dec[rows, lanes(p)]

    def outer_p(p):
        sd = landed(recv_b2, p)
        e = ef[:T, lanes(p)]
        k = kv_ref[0, 0, :, lanes(p)].astype(F32)
        dk = e * right2(nt, kv_ref[1, 0, :, lanes(p)], sd)
        dv = dot3(nn, split(k * e), sd)
        kv_out[0, 0, :, lanes(p)] = dk.astype(BF16)
        kv_out[1, 0, :, lanes(p)] = dv.astype(BF16)
        dd = right2(nn, before, split(k * dk))
        dz_ref[:T, lanes(p)] = dd * dec[:T, lanes(p)]

    def dth_part(lo, hi, p, acc):
        return acc + dot3(nt, split(dz_ref[lo * T : hi * T, lanes(p)]), split(up_ref[:, lanes(p)]))

    bulk_wait(recv_f2.at[pl.ds(0, devices - 1)], route_r.at[2])
    unrolled(steps, outer_r)
    dth_r_src[...] = unrolled(
        steps, functools.partial(dth_part, 1, 3), jnp.zeros((2 * T, RANK), F32)
    )
    exchange(dth_r_src, dth_r_land, dth_r_s, dth_r_r)
    bulk_wait(recv_b2.at[pl.ds(0, devices - 1)], route_r.at[3])
    unrolled(steps, outer_p)
    dth_p_src[...] = unrolled(steps, functools.partial(dth_part, 0, 1), jnp.zeros((T, RANK), F32))
    exchange(dth_p_src, dth_p_land, dth_p_s, dth_p_r)
    store(rkv_out, rkv_hbm_out)
    store(kv_out, kv_hbm_out)

    place = [lax.rem(me // g, n) for g, n in stages]
    size = [channels // 2]
    for g, n in stages:
        size.append(size[-1] // n)
    lands = (land0, land1, land2)
    sums = (cur1, cur2, cur3)

    def peers(stage):
        g, n = stages[stage]
        q = place[stage]
        for i in range(1, n):
            other = lax.rem(q + i, n)
            yield i, other, me + (other - q) * g

    def addend(stream, stage, q):
        rows = size[stage + 1]
        ref, base = (grad, stream * size[0]) if stage == 0 else (sums[stage - 1].at[stream], 0)
        return ref.at[pl.ds(pl.multiple_of(base + q * rows, 8), rows)]

    def rs_start(stream, stage):
        for i, other, peer in peers(stage):
            part = addend(stream, stage, other)
            ssem, rsem = rs_s.at[stream, stage, i], rs_r.at[stream, stage, place[stage]]
            remote(part, lands[stage].at[stream, place[stage]], ssem, rsem, "dp", peer).start()
            pending.append((part, ssem))

    def rs_finish(stream, stage):
        total = addend(stream, stage, place[stage])[...]
        for i, other, peer in peers(stage):
            bulk_wait(lands[stage].at[stream, other], rs_r.at[stream, stage, other])
            total = total + lands[stage][stream, other]
        sums[stage][stream] = total

    offs = [0]
    for stage in range(3):
        offs.append(offs[-1] + place[stage] * size[stage + 1])

    def piece(stream, stage, q):
        rows = size[stage + 1]
        at = stream * size[0] + offs[stage] + q * rows
        return fin.at[pl.ds(pl.multiple_of(at, 8), rows)]

    def ag_start(stream, stage):
        q = place[stage]
        mine = piece(stream, stage, q)
        if stage == 2:
            mine[...] = sums[2][stream]
        for i, other, peer in peers(stage):
            ssem, rsem = ag_s.at[stream, stage, i], ag_r.at[stream, stage, q]
            remote(mine, mine, ssem, rsem, "dp", peer).start()
            pending.append((mine, ssem))

    def ag_finish(stream, stage):
        for i, other, peer in peers(stage):
            bulk_wait(piece(stream, stage, other), ag_r.at[stream, stage, other])

    def advance(stream, step):
        if step < 3:
            rs_finish(stream, step)
        else:
            ag_finish(stream, 5 - step)
        if step < 2:
            rs_start(stream, step + 1)
        elif step < 5:
            ag_start(stream, 4 - step)
        else:
            rows = pl.ds(stream * size[0], size[0])
            store(fin.at[rows], grad_hbm_out.at[rows])

    def vec_start(stage):
        q = place[stage]
        at = sum(m for _, m in stages[:stage])
        mine = vec.at[pl.ds(3 * stage, 3)]
        for i, other, peer in peers(stage):
            ssem, rsem = vec_s.at[stage, i], vec_r.at[stage, q]
            remote(mine, vec_land.at[at + q], ssem, rsem, "dp", peer).start()
            pending.append((mine, ssem))
        vec_land[at + q] = vec[3 * stage : 3 * stage + 3]

    def vec_finish(stage):
        at = sum(m for _, m in stages[:stage])
        for i, other, peer in peers(stage):
            bulk_wait(vec_land.at[at + other], vec_r.at[stage, other])
        total = vec_land[at]
        for i in range(1, stages[stage][1]):
            total = total + vec_land[at + i]
        if stage == 2:
            vec_out[...] = total
        else:
            vec[3 * stage + 3 : 3 * stage + 6] = total

    def dh_piece(stage, q):
        g = stages[stage][0]
        return dh_land.at[pl.ds(2 * (me - lax.rem(me, g) + (q - place[stage]) * g), 2 * g)]

    def dh_start(stage):
        q = place[stage]
        mine = dh_piece(stage, q)
        for i, other, peer in peers(stage):
            remote(mine, mine, dh_s.at[stage, i], dh_r.at[stage, q], "dp", peer).start()
            pending.append((mine, dh_s.at[stage, i]))

    def dh_finish(stage):
        for i, other, peer in peers(stage):
            bulk_wait(dh_piece(stage, other), dh_r.at[stage, other])

    def up_grads(p):
        dz = dz_ref[:, lanes(p)]
        g = dot3(tn, split(th_ref[...]), split(dz))
        for n in range(blocks):
            rows = pl.ds(p * wide + n * LANES, LANES)
            grad[rows, :] = g[:, n * LANES : (n + 1) * LANES]
        vec[0, :, lanes(p)] = jnp.sum(dz, axis=0, keepdims=True)

    def down_grads(p):
        rows = pl.ds(channels + p * wide, wide)
        grad[rows, :] = dot3(tn, split(mixed[:, lanes(p)]), split(dh_ref[...]))

    def both_streams(stream, fn):
        half = (steps + 1) // 2
        unrolled(half, fn)
        rs_start(stream, 0)
        unrolled(steps - half, lambda p: fn(p + half))
        rs_start(stream + 1, 0)

    both_streams(0, up_grads)

    th = th_ref[T:, :]
    dh_ref[T:, :] = exchanged(dth_r_land, dth_r_r) * (1.0 - th * th)
    for i in range(2):
        dh_land[2 * me + i] = dh_ref[(i + 1) * T : (i + 1) * T + 1, :]
    dh_start(0)
    advance(0, 0)
    advance(1, 0)
    th = th_ref[:T, :]
    dh_ref[:T, :] = exchanged(dth_p_land, dth_p_r) * (1.0 - th * th)
    both_streams(2, down_grads)

    def x_grads(p):
        f = f_ref[:, lanes(p)]
        dm = dot3(nt, split(dh_ref[...]), split(down_ref[rows_of(p), :]))
        mix_sum = jnp.zeros((1, wide), F32)
        for i in range(3):
            x = x_of(i, p)
            g = dm[i * T : (i + 1) * T]
            ahead = jnp.where(last_row, 0.0, pltpu.roll(g, T - 1, 0))
            first = 0.0 if i == 0 else lead[i - 1 : i, lanes(p)]
            prev = jnp.where(first_row, first, pltpu.roll(x, 1, 0))
            dx = g + (ahead - g) * f
            mix_sum = mix_sum + jnp.sum(g * (prev - x), axis=0, keepdims=True)
            if i == 0:
                xp_out[0, :, lanes(p)] = dx.astype(BF16)
                xp_tail[:, lanes(p)] = dx[T - 16 :]
            else:
                xr_out[i - 1, :, lanes(p)] = dx.astype(BF16)
        vec[2, :, lanes(p)] = mix_sum

    def x_tail(late, p):
        f = f_ref[:, lanes(p)]
        more = f * dot3(nt, split(late), split(down_ref[rows_of(p), :]))[0:1]
        tail = xp_tail[:, lanes(p)]
        at_end = lax.broadcasted_iota(jnp.int32, (16, wide), 0) == 15
        xp_out[0, T - 16 :, lanes(p)] = jnp.where(at_end, tail + more, tail).astype(BF16)

    for stream, step in ((2, 0), (0, 1), (3, 0), (1, 1)):
        advance(stream, step)
    dh_finish(0)
    dh_start(1)
    by_two(steps, x_grads)
    vec_start(0)
    store(xr_out, xr_hbm_out)
    settle()
    for stream, step in ((2, 1), (0, 2), (3, 1), (1, 2)):
        advance(stream, step)
    dh_finish(1)
    dh_start(2)
    vec_finish(0)
    vec_start(1)
    settle()
    for stream, step in ((2, 2), (0, 3), (3, 2), (1, 3)):
        advance(stream, step)
    vec_finish(1)
    vec_start(2)
    dh_finish(2)
    late = dh_land[first_ref[0, me]] + dh_land[last_ref[0, me]]
    unrolled(steps, functools.partial(x_tail, jnp.broadcast_to(late, (8, RANK))))
    store(xp_out, xp_hbm_out)
    settle()
    for stream, step in ((2, 3), (0, 4), (3, 3), (1, 4)):
        advance(stream, step)
    vec_finish(2)
    store(vec_out, vec_hbm_out)
    settle()
    for stream, step in ((2, 4), (0, 5), (3, 4), (1, 5)):
        advance(stream, step)
    settle()
    advance(2, 5)
    advance(3, 5)

    for view, sem in pending:
        bulk_wait(view, sem)
    for copy in stores:
        copy.wait()


def results(pairs, *refs):
    sources, outs, held, (in_sem, out_sem) = refs[:6], refs[6:15], refs[15:21], refs[21:]
    loads = [
        pltpu.make_async_copy(a, b, in_sem.at[n]) for n, (a, b) in enumerate(zip(sources, held))
    ]
    for load in loads:
        load.start()
    moves = [[(held[n], outs[n])] for n in range(4)]
    moves.append([(held[4].at[pl.ds(pairs * LANES, pairs * LANES)], outs[4])])
    for p in range(pairs):
        lanes = pl.ds(p * LANES, LANES)
        moves[4].append((held[4].at[lanes], outs[5].at[:, lanes]))
    moves.append([(held[5].at[n], outs[6 + n]) for n in range(3)])
    copies = []
    for load, group in zip(loads, moves):
        load.wait()
        for src, dst in group:
            copies.append(pltpu.make_async_copy(src, dst, out_sem.at[len(copies)]))
            copies[-1].start()
    for copy in copies:
        copy.wait()


def per_device(
    query_text_memory,
    query_text_feed,
    reply_acceptor_memory,
    reply_feed,
    reply_cotangent_vector,
    query_placement,
    reply_parent_query,
    fading_narrowing,
    fading_widening,
    fading_anchor_rate,
    self_emphasis,
    lagged_token_fraction,
):
    devices = lax.axis_size("dp")
    ranks = lax.axis_size("mp")
    channels = query_text_feed.shape[2]
    pairs = channels // LANES
    per = HEAD * pairs // devices
    stages = stages_of(devices)
    size = [channels // 2]
    for g, n in stages:
        size.append(size[-1] // n)

    def vmem(*shape, dtype=F32):
        return pltpu.VMEM(shape, dtype)

    operands = (
        query_placement[None],
        reply_parent_query[None],
        query_text_memory,
        query_text_feed,
        reply_acceptor_memory,
        reply_feed,
        reply_cotangent_vector,
        fading_narrowing,
        fading_widening,
        fading_anchor_rate[None],
        self_emphasis[None],
        lagged_token_fraction[None],
    )
    dma = pltpu.SemaphoreType.DMA
    shapes = [
        jax.ShapeDtypeStruct(a.shape, BF16)
        for a in (reply_acceptor_memory, reply_feed, query_text_memory, query_text_feed)
    ]
    scratch = [pltpu.VMEM(a.shape, a.dtype) for a in shapes]
    scratch += [vmem(3, 1, channels)]
    scratch += [pltpu.VMEM(a.shape, a.dtype) for a in operands]
    scratch += [
        vmem(1, 2 * devices, dtype=jnp.int32),
        vmem(1, devices, dtype=jnp.int32),
        vmem(1, devices, dtype=jnp.int32),
        pltpu.SMEM((1, 2 * devices), jnp.int32),
        pltpu.SMEM((1, devices), jnp.int32),
        pltpu.SMEM((1, devices), jnp.int32),
        vmem(len(LEVELS) * T, T, dtype=BF16),
        vmem(T, len(LEVELS) * T, dtype=BF16),
        vmem(len(LEVELS) * T, min(2 * LANES, channels)),
        vmem(1, channels),
        vmem(devices, 1, channels),
        vmem(3 * T, channels),
        vmem(T, RANK),
        vmem(ranks, T, RANK),
        vmem(2 * T, RANK),
        vmem(ranks, 2 * T, RANK),
        vmem(8, channels),
        vmem(8, RANK),
        vmem(ranks, 8, RANK),
        vmem(3 * T, channels),
        vmem(3 * T, channels),
        vmem(devices, per, LANES),
        vmem(devices, per, LANES),
        vmem(devices, 2, per, LANES),
        vmem(2 * devices, per, LANES),
        vmem(devices, 2, per, LANES),
        vmem(devices, 2, per, LANES),
        vmem(devices, per, LANES),
        vmem(devices, per, LANES),
        vmem(2, T, channels),
        vmem(2, T, channels),
        vmem(3 * T, RANK),
        vmem(3 * T, channels),
        vmem(2 * T, RANK),
        vmem(ranks, 2 * T, RANK),
        vmem(T, RANK),
        vmem(ranks, T, RANK),
        vmem(3 * T, RANK),
        vmem(2 * devices, 1, RANK),
        vmem(16, channels),
        vmem(9, 1, channels),
        vmem(sum(n for _, n in stages), 3, 1, channels),
        vmem(2 * channels, RANK),
        vmem(4, size[1], RANK),
        vmem(4, size[2], RANK),
        vmem(4, size[3], RANK),
        vmem(4, stages[0][1], size[1], RANK),
        vmem(4, stages[1][1], size[2], RANK),
        vmem(4, stages[2][1], size[3], RANK),
        vmem(2 * channels, RANK),
        dma((len(operands),)),
        dma((3,)),
        dma((9,)),
        dma,
        dma,
        dma((ranks,)),
        dma((ranks,)),
        dma((ranks,)),
        dma((ranks,)),
        dma((ranks,)),
        dma((ranks,)),
        dma((4,)),
        dma((4,)),
        dma((ranks,)),
        dma((ranks,)),
        dma((ranks,)),
        dma((ranks,)),
        dma((3, 8)),
        dma((3, 8)),
        dma((3, 8)),
        dma((3, 8)),
        dma((4, 3, 8)),
        dma((4, 3, 8)),
        dma((4, 3, 8)),
        dma((4, 3, 8)),
    ]
    far = pl.BlockSpec(memory_space=pltpu.HBM)
    moved = pl.pallas_call(
        functools.partial(body, devices, ranks, channels),
        out_shape=(
            *shapes,
            jax.ShapeDtypeStruct((2 * channels, RANK), F32),
            jax.ShapeDtypeStruct((3, 1, channels), F32),
        ),
        in_specs=[far] * len(operands),
        out_specs=[far] * 6,
        scratch_shapes=scratch,
        compiler_params=pltpu.CompilerParams(
            collective_id=0, has_side_effects=True, vmem_limit_bytes=VMEM
        ),
    )(*operands)
    rkv, xr, kv, xp, down, up, *vectors = pl.pallas_call(
        functools.partial(results, pairs),
        out_shape=(
            *shapes,
            jax.ShapeDtypeStruct(fading_narrowing.shape, F32),
            jax.ShapeDtypeStruct(fading_widening.shape, F32),
            *[jax.ShapeDtypeStruct((1, channels), F32)] * 3,
        ),
        in_specs=[far] * 6,
        out_specs=[far] * 9,
        scratch_shapes=[pltpu.VMEM(a.shape, a.dtype) for a in moved]
        + [dma((6,)), dma((8 + pairs,))],
        compiler_params=pltpu.CompilerParams(vmem_limit_bytes=VMEM),
    )(*moved)
    return rkv, xr, kv, xp, down, up, *[v.reshape(channels) for v in vectors]


def solution(mesh):
    in_specs = (
        P(None, "dp", None, "mp"),
        P("dp", None, "mp"),
        P(None, "dp", None, "mp"),
        P("dp", None, "mp"),
        P("dp", None, "mp"),
        P(),
        P(),
        P("mp", None),
        P(None, "mp"),
        P("mp"),
        P("mp"),
        P("mp"),
    )
    out_specs = (
        P(None, "dp", None, "mp"),
        P("dp", None, "mp"),
        P(None, "dp", None, "mp"),
        P("dp", None, "mp"),
        P("mp", None),
        P(None, "mp"),
        P("mp"),
        P("mp"),
        P("mp"),
    )
    return jax.shard_map(
        per_device, mesh=mesh, in_specs=in_specs, out_specs=out_specs, check_vma=False
    )
```

```python
import functools

import jax
import jax.numpy as jnp
from jax import lax
from jax.experimental import pallas as pl
from jax.experimental.pallas import tpu as pltpu
from jax.sharding import PartitionSpec as P

HEAD = 64
T = 64
LANES = 128
RANK = 128
VMEM = 63 * 1024 * 1024
LEVELS = (32, 16, 8, 4, 2, 1)
MESH = pl.DeviceIdType.MESH
F32 = jnp.float32
BF16 = jnp.bfloat16


def stages_of(devices):
    if devices == 64:
        return ((1, 2), (2, 4), (8, 8))
    return ((1, 2), (2, 2), (4, devices // 4))


def nn(a, b):
    return lax.dot_general(a, b, (((1,), (0,)), ((), ())), preferred_element_type=F32)


def nt(a, b):
    return lax.dot_general(a, b, (((1,), (1,)), ((), ())), preferred_element_type=F32)


def tn(a, b):
    return lax.dot_general(a, b, (((0,), (0,)), ((), ())), preferred_element_type=F32)


def split(x):
    hi = x.astype(BF16)
    return hi, (x - hi.astype(F32)).astype(BF16)


def split3(x):
    hi = x.astype(BF16)
    rest = x - hi.astype(F32)
    mid = rest.astype(BF16)
    return hi, mid, (rest - mid.astype(F32)).astype(BF16)


def dot3(dot, a, b):
    return dot(a[0], b[0]) + (dot(a[0], b[1]) + dot(a[1], b[0]))


def left2(dot, a, b):
    return dot(a[0], b) + dot(a[1], b)


def right2(dot, a, b):
    return dot(a, b[0]) + dot(a, b[1])


def block_diag(x):
    head = lax.broadcasted_iota(jnp.int32, x.shape, 1) // HEAD
    zero = jnp.zeros_like(x)
    return jnp.concatenate(
        [jnp.where(head == h, x, zero) for h in range(x.shape[1] // HEAD)], axis=0
    )


def pack_diag(m):
    n = m.shape[1] // HEAD
    head = lax.broadcasted_iota(jnp.int32, (HEAD, m.shape[1]), 1) // HEAD
    out = m[:HEAD]
    for h in range(1, n):
        out = jnp.where(head == h, m[h * HEAD : (h + 1) * HEAD], out)
    return out


def body(
    devices,
    ranks,
    channels,
    place_hbm,
    parent_hbm,
    kv_hbm,
    xp_hbm,
    rkv_hbm,
    xr_hbm,
    dy_hbm,
    down_hbm,
    up_hbm,
    base_hbm,
    u_hbm,
    f_hbm,
    rkv_hbm_out,
    xr_hbm_out,
    kv_hbm_out,
    xp_hbm_out,
    grad_hbm_out,
    vec_hbm_out,
    rkv_out,
    xr_out,
    kv_out,
    xp_out,
    vec_out,
    place_ref,
    parent_ref,
    kv_ref,
    xp_ref,
    rkv_ref,
    xr_ref,
    dy_ref,
    down_ref,
    up_ref,
    base_ref,
    u_ref,
    f_ref,
    owner_vec,
    first_vec,
    last_vec,
    owner_ref,
    first_ref,
    last_ref,
    gaps_ref,
    gaps_t_ref,
    masks_ref,
    row_src,
    row_land,
    mixed,
    hid_p,
    hid_p_land,
    hid_r,
    hid_r_land,
    lead,
    lead_hid,
    lead_land,
    dec,
    ef,
    send_f1,
    recv_f1,
    send_b1,
    recv_b1,
    send_f2,
    recv_f2,
    send_b2,
    recv_b2,
    dr_loc,
    dd_loc,
    th_ref,
    dz_ref,
    dth_r_src,
    dth_r_land,
    dth_p_src,
    dth_p_land,
    dh_ref,
    dh_land,
    xp_tail,
    vec,
    vec_land,
    grad,
    cur1,
    cur2,
    cur3,
    land0,
    land1,
    land2,
    fin,
    in_sem,
    index_sem,
    out_sem,
    row_s,
    row_r,
    hid_p_s,
    hid_p_r,
    hid_r_s,
    hid_r_r,
    lead_s,
    lead_r,
    route_s,
    route_r,
    dth_r_s,
    dth_r_r,
    dth_p_s,
    dth_p_r,
    dh_s,
    dh_r,
    vec_s,
    vec_r,
    rs_s,
    rs_r,
    ag_s,
    ag_r,
):
    me = lax.axis_index("dp")
    rank = lax.axis_index("mp")
    wide = min(2 * LANES, channels)
    blocks = wide // LANES
    steps = channels // wide
    per = HEAD * (channels // LANES) // devices
    dests = HEAD // per
    stages = stages_of(devices)

    def lanes(p):
        if isinstance(p, int):
            return pl.ds(p * wide, wide)
        return pl.ds(pl.multiple_of(p * wide, LANES), wide)

    rows_of = lanes

    def loop(n, fn, init=None):
        if init is None:
            lax.fori_loop(0, n, lambda i, c: (fn(i), c)[1], 0)
            return None
        return lax.fori_loop(0, n, fn, init)

    def unrolled(n, fn, init=None):
        for i in range(n):
            init = fn(i) if init is None else fn(i, init)
        return init

    def by_two(n, fn):
        if n % 2:
            return loop(n, fn)
        return loop(n // 2, lambda i: (fn(2 * i), fn(2 * i + 1)))

    def remote(src, dst, ssem, rsem, axis, peer):
        return pltpu.make_async_remote_copy(
            src_ref=src,
            dst_ref=dst,
            send_sem=ssem,
            recv_sem=rsem,
            device_id={axis: peer},
            device_id_type=MESH,
        )

    def nth_peer(i):
        k = (i + 1) // 2
        return lax.rem(me + devices // 2 + k * (1 - 2 * (i % 2)), devices)

    def bulk_wait(view, sem):
        pltpu.make_async_copy(view, view, sem).wait()

    pending = []
    settled = [0]

    def settle():
        for view, sem in pending[: settled[0]]:
            bulk_wait(view, sem)
        del pending[: settled[0]]
        settled[0] = len(pending)

    barrier = pltpu.get_barrier_semaphore()

    def greet(i):
        pl.semaphore_signal(
            barrier, inc=1, device_id={"dp": lax.rem(me + 1 + i, devices)}, device_id_type=MESH
        )

    fetches = [
        pltpu.make_async_copy(src, dst, in_sem.at[n])
        for n, (src, dst) in enumerate(
            (
                (xp_hbm, xp_ref),
                (xr_hbm, xr_ref),
                (f_hbm, f_ref),
                (down_hbm, down_ref),
                (up_hbm, up_ref),
                (base_hbm, base_ref),
                (kv_hbm, kv_ref),
                (rkv_hbm, rkv_ref),
                (dy_hbm, dy_ref),
                (u_hbm, u_ref),
                (place_hbm, place_ref),
                (parent_hbm, parent_ref),
            )
        )
    ]
    for fetch in fetches:
        fetch.start()

    for i in range(1, ranks):
        pl.semaphore_signal(
            barrier, inc=1, device_id={"mp": lax.rem(rank + i, ranks)}, device_id_type=MESH
        )
    loop(devices - 1, greet)

    stores = []

    def store(src, dst):
        copy = pltpu.make_async_copy(src, dst, out_sem.at[len(stores)])
        copy.start()
        stores.append(copy)

    first_row = lax.broadcasted_iota(jnp.int32, (T, wide), 0) == 0
    last_row = lax.broadcasted_iota(jnp.int32, (T, wide), 0) == T - 1

    def x_of(i, p):
        return (xp_ref[0, :, lanes(p)] if i == 0 else xr_ref[i - 1, :, lanes(p)]).astype(F32)

    def mix(p, acc):
        f = f_ref[:, lanes(p)]
        parts = []
        for i in range(3):
            x = x_of(i, p)
            prev = jnp.where(first_row, 0.0, pltpu.roll(x, 1, 0))
            m = x + (prev - x) * f
            mixed[i * T : (i + 1) * T, lanes(p)] = m
            parts.append(m)
        return acc + dot3(nn, split(jnp.concatenate(parts, axis=0)), split(down_ref[rows_of(p), :]))

    for fetch in fetches[:4]:
        fetch.wait()
    row_src[...] = xp_ref[0, T - 16 :, :].astype(F32)[15:16]
    partial = unrolled(steps, mix, jnp.zeros((3 * T, RANK), F32))
    hid_p[...] = partial[:T]
    hid_r[...] = partial[T:]
    for fetch in fetches[4:]:
        fetch.wait()
    def column(row):
        n = row.shape[1]
        diagonal = lax.broadcasted_iota(jnp.int32, (n, n), 0) == lax.broadcasted_iota(
            jnp.int32, (n, n), 1
        )
        return jnp.sum(jnp.where(diagonal, row, 0), axis=1, keepdims=True)

    placed, parents = place_ref[...], parent_ref[...]
    pairs_at = (devices, 2 * devices)
    match = column(placed) == parents
    slot = lax.broadcasted_iota(jnp.int32, pairs_at, 0)
    owner_vec[...] = jnp.max(jnp.where(match, slot, 0), axis=0, keepdims=True)
    match = column(parents) == placed
    response = lax.broadcasted_iota(jnp.int32, pairs_at[::-1], 0)
    first_vec[...] = jnp.min(
        jnp.where(match, response, 2 * devices - 1), axis=0, keepdims=True
    )
    last_vec[...] = jnp.max(jnp.where(match, response, 0), axis=0, keepdims=True)
    indices = [
        pltpu.make_async_copy(src, dst, index_sem.at[n])
        for n, (src, dst) in enumerate(
            ((owner_vec, owner_ref), (first_vec, first_ref), (last_vec, last_ref))
        )
    ]
    for copy in indices:
        copy.start()
    pl.semaphore_wait(barrier, devices - 1 + ranks - 1)

    def exchange(src, land, ssem, rsem):
        for i in range(1, ranks):
            peer = lax.rem(rank + i, ranks)
            remote(src, land.at[rank], ssem.at[i], rsem.at[rank], "mp", peer).start()
            pending.append((src, ssem.at[i]))
        land[rank] = src[...]

    def exchanged(land, rsem):
        for i in range(1, ranks):
            source = lax.rem(rank + i, ranks)
            bulk_wait(land.at[source], rsem.at[source])
        total = land[0]
        for i in range(1, ranks):
            total = total + land[i]
        return total

    def send_row(i):
        peer = nth_peer(i)
        remote(row_src, row_land.at[me], row_s, row_r, "dp", peer).start()

    exchange(hid_p, hid_p_land, hid_p_s, hid_p_r)
    exchange(hid_r, hid_r_land, hid_r_s, hid_r_r)
    loop(devices - 1, send_row)
    pending.append((row_land.at[pl.ds(0, devices - 1)], row_s))
    row_land[me] = row_src[...]
    t_sq = lax.broadcasted_iota(jnp.int32, (T, T), 0)
    j_sq = lax.broadcasted_iota(jnp.int32, (T, T), 1)
    before = (j_sq < t_sq).astype(F32).astype(BF16)
    suffix = (j_sq > t_sq).astype(F32).astype(BF16)

    def exact(mask, x):
        hi, mid, low = split3(x)
        return nn(mask, hi) + (nn(mask, mid) + nn(mask, low))

    def decays(lo, hi, p):
        z = dot3(nn, split(th_ref[lo * T : hi * T, :]), split(up_ref[:, lanes(p)]))
        d = -jnp.exp(z + base_ref[:, lanes(p)])
        dec[lo * T : hi * T, lanes(p)] = d
        for i in range(lo, hi):
            at = (i - lo) * T
            e = jnp.exp(exact(suffix if i == 0 else before, d[at : at + T]))
            ef[i * T : (i + 1) * T, lanes(p)] = e
            if i == 0:
                a, b = kv_ref[0, 0, :, lanes(p)], kv_ref[1, 0, :, lanes(p)]
            else:
                a, b = rkv_ref[0, i - 1, :, lanes(p)], dy_ref[i - 1, :, lanes(p)]
            packed = pack_diag(left2(tn, split(a.astype(F32) * e), b))
            for n in range(blocks):
                part = packed[:, n * LANES : (n + 1) * LANES].reshape(dests, per, LANES)
                at = pl.ds((p * blocks + n) * dests, dests)
                if i == 0:
                    send_f1[at] = part
                else:
                    send_b1[at, i - 1] = part

    def route(n, src, dst_of, fill=None):
        def send(i):
            peer = nth_peer(i)
            if fill is not None:
                fill(peer)
            remote(src.at[peer], dst_of(me), route_s.at[n], route_r.at[n], "dp", peer).start()

        loop(devices - 1, send)
        pending.append((src.at[pl.ds(0, devices - 1)], route_s.at[n]))

    th_ref[:T, :] = jnp.tanh(exchanged(hid_p_land, hid_p_r))
    unrolled(steps, functools.partial(decays, 0, 1))
    route(0, send_f1, lambda m: recv_f1.at[m])
    recv_f1[me] = send_f1[me]

    bulk_wait(row_land.at[pl.ds(0, devices - 1)], row_r)
    for copy in indices:
        copy.wait()
    lead_rows = [row_land[owner_ref[0, 2 * me + i]] for i in range(2)]
    row8 = lax.broadcasted_iota(jnp.int32, (8, channels), 0)
    lead[...] = jnp.where(row8 == 0, lead_rows[0], jnp.where(row8 == 1, lead_rows[1], 0.0))

    def lead_mix(p, acc):
        fl = f_ref[:, lanes(p)] * lead[:, lanes(p)]
        for i in range(2):
            at = (i + 1) * T
            mixed[at : at + 1, lanes(p)] = mixed[at : at + 1, lanes(p)] + fl[i : i + 1]
        return acc + dot3(nn, split(fl), split(down_ref[rows_of(p), :]))

    lead_hid[...] = unrolled(steps, lead_mix, jnp.zeros((8, RANK), F32))
    exchange(lead_hid, lead_land, lead_s, lead_r)
    hidden = exchanged(hid_r_land, hid_r_r)
    th_ref[T:, :] = jnp.tanh(hidden)
    extra = exchanged(lead_land, lead_r)
    for i in range(2):
        at = (i + 1) * T
        th_ref[at : at + 1, :] = jnp.tanh(hidden[i * T : i * T + 1] + extra[i : i + 1])
    unrolled(steps, functools.partial(decays, 1, 3))
    route(1, send_b1, lambda m: recv_b1.at[pl.ds(2 * m, 2)])
    recv_b1[pl.ds(2 * me, 2)] = send_b1[me]

    bulk_wait(recv_f1.at[pl.ds(0, devices - 1)], route_r.at[0])

    def shuffle_f(n):
        send_f2[n, 0] = recv_f1[owner_ref[0, 2 * n]]
        send_f2[n, 1] = recv_f1[owner_ref[0, 2 * n + 1]]

    route(2, send_f2, lambda m: recv_f2.at[m], shuffle_f)
    shuffle_f(me)
    recv_f2[me] = send_f2[me]

    def gap_mask(shape, t_axis, level):
        t = lax.broadcasted_iota(jnp.int32, shape, t_axis)
        j = lax.broadcasted_iota(jnp.int32, shape, 1 - t_axis)
        b = LEVELS[level]
        second = (t & b) != 0
        late = second & (j >= (t & -b)) & (j < t)
        early = ~second & (j > t) & (j <= (t | (b - 1)))
        return (late | early).astype(F32).astype(BF16)

    for level in range(len(LEVELS)):
        gaps_ref[level * T : (level + 1) * T, :] = gap_mask((T, T), 0, level)
    for level in range(0, len(LEVELS), 2):
        both = [gap_mask((T, T), 1, level + n) for n in range(2)]
        gaps_t_ref[:, level * T : (level + 2) * T] = jnp.concatenate(both, axis=1)
    t_row = lax.broadcasted_iota(jnp.int32, (T, wide), 0)
    s_col = lax.broadcasted_iota(jnp.int32, (T, wide), 1) & (T - 1)
    apart = t_row ^ s_col
    for level, b in enumerate(LEVELS):
        masks_ref[level * T : (level + 1) * T, :] = ((apart >= b) & (apart < 2 * b)).astype(F32)

    ones_block = (
        (
            lax.broadcasted_iota(jnp.int32, (wide, wide), 0) // HEAD
            == lax.broadcasted_iota(jnp.int32, (wide, wide), 1) // HEAD
        )
        .astype(F32)
        .astype(BF16)
    )
    deep = len(LEVELS) - 1

    def inner(i, p):
        cols = lanes(p)
        rb, kb, vb = (rkv_ref[n, i, :, cols] for n in range(3))
        yb = dy_ref[i, :, cols]
        r, k, v, y = (a.astype(F32) for a in (rb, kb, vb, yb))
        d = dec[(i + 1) * T : (i + 2) * T, cols]
        u = u_ref[:, cols]
        y_diag = block_diag(yb)
        sym = jnp.where(t_row > s_col, nt(yb, block_diag(vb)), nt(vb, y_diag))
        gap = exact(gaps_ref[: deep * T, :], d)
        att = jnp.zeros((T, wide), F32)
        dr = jnp.zeros((T, wide), F32)
        dk = jnp.zeros((T, wide), F32)
        dgaps = []
        for level, b in enumerate(LEVELS):
            second = (t_row & b) != 0
            mask = masks_ref[level * T : (level + 1) * T, :]
            side = jnp.where(second, r, k)
            if level == deep:
                w = side.astype(BF16)
                wd = block_diag(w)
                att = att + mask * nt(w, wd)
                g = left2(nn, split(mask * sym), wd)
            else:
                x = jnp.exp(gap[level * T : (level + 1) * T])
                w = side * x
                ws = split(w)
                wd = tuple(block_diag(a) for a in ws)
                att = att + mask * dot3(nt, ws, wd)
                dw = dot3(nn, split(mask * sym), wd)
                dgaps.append(w * dw)
                g = x * dw
            dr = dr + jnp.where(second, g, 0.0)
            dk = dk + jnp.where(second, 0.0, g)
        dgap = jnp.concatenate(dgaps, axis=0)
        dd_loc[i, :, cols] = right2(nn, gaps_t_ref[:, : deep * T], split(dgap))
        self_a = left2(nn, split(r * u * k), ones_block)
        self_b = left2(nn, split(y * v), ones_block)
        dv = left2(nn, split(jnp.where(s_col > t_row, att, 0.0)), y_diag) + self_a * y
        dr_loc[i, :, cols] = dr + u * k * self_b
        rkv_out[1, i, :, cols] = (dk + u * r * self_b).astype(BF16)
        rkv_out[2, i, :, cols] = dv.astype(BF16)
        part = jnp.sum(r * k * self_b, axis=0, keepdims=True)
        if i == 0:
            vec[1, :, cols] = part
        else:
            vec[1, :, cols] = vec[1, :, cols] + part

    loop(steps, functools.partial(inner, 0))
    bulk_wait(recv_b1.at[pl.ds(0, 2 * (devices - 1))], route_r.at[1])

    def shuffle_b(n):
        send_b2[n] = recv_b1[first_ref[0, n]] + recv_b1[last_ref[0, n]]

    route(3, send_b2, lambda m: recv_b2.at[m], shuffle_b)
    shuffle_b(me)
    recv_b2[me] = send_b2[me]
    loop(steps, functools.partial(inner, 1))

    def landed(ref, p, *i):
        parts = [
            ref[(pl.ds((p * blocks + n) * dests, dests), *i)].reshape(HEAD, LANES)
            for n in range(blocks)
        ]
        return tuple(block_diag(a) for a in split(jnp.concatenate(parts, axis=1)))

    def outer_r(p):
        for i in range(2):
            sd = landed(recv_f2, p, i)
            rows = slice((i + 1) * T, (i + 2) * T)
            r = rkv_ref[0, i, :, lanes(p)].astype(F32)
            drs = ef[rows, lanes(p)] * right2(nt, dy_ref[i, :, lanes(p)], sd)
            rkv_out[0, i, :, lanes(p)] = (dr_loc[i, :, lanes(p)] + drs).astype(BF16)
            dd = right2(nn, suffix, split(r * drs)) + dd_loc[i, :, lanes(p)]
            dz_ref[rows, lanes(p)] = dd * dec[rows, lanes(p)]

    def outer_p(p):
        sd = landed(recv_b2, p)
        e = ef[:T, lanes(p)]
        k = kv_ref[0, 0, :, lanes(p)].astype(F32)
        dk = e * right2(nt, kv_ref[1, 0, :, lanes(p)], sd)
        dv = dot3(nn, split(k * e), sd)
        kv_out[0, 0, :, lanes(p)] = dk.astype(BF16)
        kv_out[1, 0, :, lanes(p)] = dv.astype(BF16)
        dd = right2(nn, before, split(k * dk))
        dz_ref[:T, lanes(p)] = dd * dec[:T, lanes(p)]

    def dth_part(lo, hi, p, acc):
        return acc + dot3(nt, split(dz_ref[lo * T : hi * T, lanes(p)]), split(up_ref[:, lanes(p)]))

    bulk_wait(recv_f2.at[pl.ds(0, devices - 1)], route_r.at[2])
    unrolled(steps, outer_r)
    dth_r_src[...] = unrolled(
        steps, functools.partial(dth_part, 1, 3), jnp.zeros((2 * T, RANK), F32)
    )
    exchange(dth_r_src, dth_r_land, dth_r_s, dth_r_r)
    bulk_wait(recv_b2.at[pl.ds(0, devices - 1)], route_r.at[3])
    unrolled(steps, outer_p)
    dth_p_src[...] = unrolled(steps, functools.partial(dth_part, 0, 1), jnp.zeros((T, RANK), F32))
    exchange(dth_p_src, dth_p_land, dth_p_s, dth_p_r)
    store(rkv_out, rkv_hbm_out)
    store(kv_out, kv_hbm_out)

    place = [lax.rem(me // g, n) for g, n in stages]
    size = [channels // 2]
    for g, n in stages:
        size.append(size[-1] // n)
    lands = (land0, land1, land2)
    sums = (cur1, cur2, cur3)

    def peers(stage):
        g, n = stages[stage]
        q = place[stage]
        for i in range(1, n):
            other = lax.rem(q + i, n)
            yield i, other, me + (other - q) * g

    def addend(stream, stage, q):
        rows = size[stage + 1]
        ref, base = (grad, stream * size[0]) if stage == 0 else (sums[stage - 1].at[stream], 0)
        return ref.at[pl.ds(pl.multiple_of(base + q * rows, 8), rows)]

    def rs_start(stream, stage):
        for i, other, peer in peers(stage):
            part = addend(stream, stage, other)
            ssem, rsem = rs_s.at[stream, stage, i], rs_r.at[stream, stage, place[stage]]
            remote(part, lands[stage].at[stream, place[stage]], ssem, rsem, "dp", peer).start()
            pending.append((part, ssem))

    def rs_finish(stream, stage):
        total = addend(stream, stage, place[stage])[...]
        for i, other, peer in peers(stage):
            bulk_wait(lands[stage].at[stream, other], rs_r.at[stream, stage, other])
            total = total + lands[stage][stream, other]
        sums[stage][stream] = total

    offs = [0]
    for stage in range(3):
        offs.append(offs[-1] + place[stage] * size[stage + 1])

    def piece(stream, stage, q):
        rows = size[stage + 1]
        at = stream * size[0] + offs[stage] + q * rows
        return fin.at[pl.ds(pl.multiple_of(at, 8), rows)]

    def ag_start(stream, stage):
        q = place[stage]
        mine = piece(stream, stage, q)
        if stage == 2:
            mine[...] = sums[2][stream]
        for i, other, peer in peers(stage):
            ssem, rsem = ag_s.at[stream, stage, i], ag_r.at[stream, stage, q]
            remote(mine, mine, ssem, rsem, "dp", peer).start()
            pending.append((mine, ssem))

    def ag_finish(stream, stage):
        for i, other, peer in peers(stage):
            bulk_wait(piece(stream, stage, other), ag_r.at[stream, stage, other])

    def advance(stream, step):
        if step < 3:
            rs_finish(stream, step)
        else:
            ag_finish(stream, 5 - step)
        if step < 2:
            rs_start(stream, step + 1)
        elif step < 5:
            ag_start(stream, 4 - step)
        else:
            rows = pl.ds(stream * size[0], size[0])
            store(fin.at[rows], grad_hbm_out.at[rows])

    def vec_start(stage):
        q = place[stage]
        at = sum(m for _, m in stages[:stage])
        mine = vec.at[pl.ds(3 * stage, 3)]
        for i, other, peer in peers(stage):
            ssem, rsem = vec_s.at[stage, i], vec_r.at[stage, q]
            remote(mine, vec_land.at[at + q], ssem, rsem, "dp", peer).start()
            pending.append((mine, ssem))
        vec_land[at + q] = vec[3 * stage : 3 * stage + 3]

    def vec_finish(stage):
        at = sum(m for _, m in stages[:stage])
        for i, other, peer in peers(stage):
            bulk_wait(vec_land.at[at + other], vec_r.at[stage, other])
        total = vec_land[at]
        for i in range(1, stages[stage][1]):
            total = total + vec_land[at + i]
        if stage == 2:
            vec_out[...] = total
        else:
            vec[3 * stage + 3 : 3 * stage + 6] = total

    def dh_piece(stage, q):
        g = stages[stage][0]
        return dh_land.at[pl.ds(2 * (me - lax.rem(me, g) + (q - place[stage]) * g), 2 * g)]

    def dh_start(stage):
        q = place[stage]
        mine = dh_piece(stage, q)
        for i, other, peer in peers(stage):
            remote(mine, mine, dh_s.at[stage, i], dh_r.at[stage, q], "dp", peer).start()
            pending.append((mine, dh_s.at[stage, i]))

    def dh_finish(stage):
        for i, other, peer in peers(stage):
            bulk_wait(dh_piece(stage, other), dh_r.at[stage, other])

    def up_grads(p):
        dz = dz_ref[:, lanes(p)]
        g = dot3(tn, split(th_ref[...]), split(dz))
        for n in range(blocks):
            rows = pl.ds(p * wide + n * LANES, LANES)
            grad[rows, :] = g[:, n * LANES : (n + 1) * LANES]
        vec[0, :, lanes(p)] = jnp.sum(dz, axis=0, keepdims=True)

    def down_of(p, lo, hi):
        return dot3(
            tn, split(mixed[lo * T : hi * T, lanes(p)]), split(dh_ref[lo * T : hi * T, :])
        )

    def down_early(p):
        grad[pl.ds(channels + p * wide, wide), :] = down_of(p, 1, 3)

    def down_grads(p):
        rows = pl.ds(channels + p * wide, wide)
        grad[rows, :] = grad[rows, :] + down_of(p, 0, 1)

    def both_streams(stream, fn):
        half = (steps + 1) // 2
        unrolled(half, fn)
        rs_start(stream, 0)
        unrolled(steps - half, lambda p: fn(p + half))
        rs_start(stream + 1, 0)

    both_streams(0, up_grads)

    th = th_ref[T:, :]
    dh_ref[T:, :] = exchanged(dth_r_land, dth_r_r) * (1.0 - th * th)
    for i in range(2):
        dh_land[2 * me + i] = dh_ref[(i + 1) * T : (i + 1) * T + 1, :]
    dh_start(0)
    advance(0, 0)
    advance(1, 0)
    unrolled(steps, down_early)
    th = th_ref[:T, :]
    dh_ref[:T, :] = exchanged(dth_p_land, dth_p_r) * (1.0 - th * th)
    both_streams(2, down_grads)

    def x_grads(p):
        f = f_ref[:, lanes(p)]
        dm = dot3(nt, split(dh_ref[...]), split(down_ref[rows_of(p), :]))
        mix_sum = jnp.zeros((1, wide), F32)
        for i in range(3):
            x = x_of(i, p)
            g = dm[i * T : (i + 1) * T]
            ahead = jnp.where(last_row, 0.0, pltpu.roll(g, T - 1, 0))
            first = 0.0 if i == 0 else lead[i - 1 : i, lanes(p)]
            prev = jnp.where(first_row, first, pltpu.roll(x, 1, 0))
            dx = g + (ahead - g) * f
            mix_sum = mix_sum + jnp.sum(g * (prev - x), axis=0, keepdims=True)
            if i == 0:
                xp_out[0, :, lanes(p)] = dx.astype(BF16)
                xp_tail[:, lanes(p)] = dx[T - 16 :]
            else:
                xr_out[i - 1, :, lanes(p)] = dx.astype(BF16)
        vec[2, :, lanes(p)] = mix_sum

    def x_tail(late, p):
        f = f_ref[:, lanes(p)]
        more = f * dot3(nt, split(late), split(down_ref[rows_of(p), :]))[0:1]
        tail = xp_tail[:, lanes(p)]
        at_end = lax.broadcasted_iota(jnp.int32, (16, wide), 0) == 15
        xp_out[0, T - 16 :, lanes(p)] = jnp.where(at_end, tail + more, tail).astype(BF16)

    for stream, step in ((2, 0), (0, 1), (3, 0), (1, 1)):
        advance(stream, step)
    dh_finish(0)
    dh_start(1)
    loop(steps, x_grads)
    vec_start(0)
    store(xr_out, xr_hbm_out)
    settle()
    for stream, step in ((2, 1), (0, 2), (3, 1), (1, 2)):
        advance(stream, step)
    dh_finish(1)
    dh_start(2)
    vec_finish(0)
    vec_start(1)
    settle()
    for stream, step in ((2, 2), (0, 3), (3, 2), (1, 3)):
        advance(stream, step)
    vec_finish(1)
    vec_start(2)
    dh_finish(2)
    late = dh_land[first_ref[0, me]] + dh_land[last_ref[0, me]]
    unrolled(steps, functools.partial(x_tail, jnp.broadcast_to(late, (8, RANK))))
    store(xp_out, xp_hbm_out)
    settle()
    for stream, step in ((2, 3), (0, 4), (3, 3), (1, 4)):
        advance(stream, step)
    vec_finish(2)
    store(vec_out, vec_hbm_out)
    settle()
    for stream, step in ((2, 4), (0, 5), (3, 4), (1, 5)):
        advance(stream, step)
    settle()
    advance(2, 5)
    advance(3, 5)

    for view, sem in pending:
        bulk_wait(view, sem)
    for copy in stores:
        copy.wait()


def results(pairs, *refs):
    sources, outs, held, (in_sem, out_sem) = refs[:6], refs[6:15], refs[15:21], refs[21:]
    loads = [
        pltpu.make_async_copy(a, b, in_sem.at[n]) for n, (a, b) in enumerate(zip(sources, held))
    ]
    for load in loads:
        load.start()
    moves = [[(held[n], outs[n])] for n in range(4)]
    moves.append([(held[4].at[pl.ds(pairs * LANES, pairs * LANES)], outs[4])])
    for p in range(pairs):
        lanes = pl.ds(p * LANES, LANES)
        moves[4].append((held[4].at[lanes], outs[5].at[:, lanes]))
    moves.append([(held[5].at[n], outs[6 + n]) for n in range(3)])
    copies = []
    for load, group in zip(loads, moves):
        load.wait()
        for src, dst in group:
            copies.append(pltpu.make_async_copy(src, dst, out_sem.at[len(copies)]))
            copies[-1].start()
    for copy in copies:
        copy.wait()


def per_device(
    query_text_memory,
    query_text_feed,
    reply_acceptor_memory,
    reply_feed,
    reply_cotangent_vector,
    query_placement,
    reply_parent_query,
    fading_narrowing,
    fading_widening,
    fading_anchor_rate,
    self_emphasis,
    lagged_token_fraction,
):
    devices = lax.axis_size("dp")
    ranks = lax.axis_size("mp")
    channels = query_text_feed.shape[2]
    pairs = channels // LANES
    per = HEAD * pairs // devices
    stages = stages_of(devices)
    size = [channels // 2]
    for g, n in stages:
        size.append(size[-1] // n)

    def vmem(*shape, dtype=F32):
        return pltpu.VMEM(shape, dtype)

    operands = (
        query_placement[None],
        reply_parent_query[None],
        query_text_memory,
        query_text_feed,
        reply_acceptor_memory,
        reply_feed,
        reply_cotangent_vector,
        fading_narrowing,
        fading_widening,
        fading_anchor_rate[None],
        self_emphasis[None],
        lagged_token_fraction[None],
    )
    dma = pltpu.SemaphoreType.DMA
    shapes = [
        jax.ShapeDtypeStruct(a.shape, BF16)
        for a in (reply_acceptor_memory, reply_feed, query_text_memory, query_text_feed)
    ]
    scratch = [pltpu.VMEM(a.shape, a.dtype) for a in shapes]
    scratch += [vmem(3, 1, channels)]
    scratch += [pltpu.VMEM(a.shape, a.dtype) for a in operands]
    scratch += [
        vmem(1, 2 * devices, dtype=jnp.int32),
        vmem(1, devices, dtype=jnp.int32),
        vmem(1, devices, dtype=jnp.int32),
        pltpu.SMEM((1, 2 * devices), jnp.int32),
        pltpu.SMEM((1, devices), jnp.int32),
        pltpu.SMEM((1, devices), jnp.int32),
        vmem(len(LEVELS) * T, T, dtype=BF16),
        vmem(T, len(LEVELS) * T, dtype=BF16),
        vmem(len(LEVELS) * T, min(2 * LANES, channels)),
        vmem(1, channels),
        vmem(devices, 1, channels),
        vmem(3 * T, channels),
        vmem(T, RANK),
        vmem(ranks, T, RANK),
        vmem(2 * T, RANK),
        vmem(ranks, 2 * T, RANK),
        vmem(8, channels),
        vmem(8, RANK),
        vmem(ranks, 8, RANK),
        vmem(3 * T, channels),
        vmem(3 * T, channels),
        vmem(devices, per, LANES),
        vmem(devices, per, LANES),
        vmem(devices, 2, per, LANES),
        vmem(2 * devices, per, LANES),
        vmem(devices, 2, per, LANES),
        vmem(devices, 2, per, LANES),
        vmem(devices, per, LANES),
        vmem(devices, per, LANES),
        vmem(2, T, channels),
        vmem(2, T, channels),
        vmem(3 * T, RANK),
        vmem(3 * T, channels),
        vmem(2 * T, RANK),
        vmem(ranks, 2 * T, RANK),
        vmem(T, RANK),
        vmem(ranks, T, RANK),
        vmem(3 * T, RANK),
        vmem(2 * devices, 1, RANK),
        vmem(16, channels),
        vmem(9, 1, channels),
        vmem(sum(n for _, n in stages), 3, 1, channels),
        vmem(2 * channels, RANK),
        vmem(4, size[1], RANK),
        vmem(4, size[2], RANK),
        vmem(4, size[3], RANK),
        vmem(4, stages[0][1], size[1], RANK),
        vmem(4, stages[1][1], size[2], RANK),
        vmem(4, stages[2][1], size[3], RANK),
        vmem(2 * channels, RANK),
        dma((len(operands),)),
        dma((3,)),
        dma((9,)),
        dma,
        dma,
        dma((ranks,)),
        dma((ranks,)),
        dma((ranks,)),
        dma((ranks,)),
        dma((ranks,)),
        dma((ranks,)),
        dma((4,)),
        dma((4,)),
        dma((ranks,)),
        dma((ranks,)),
        dma((ranks,)),
        dma((ranks,)),
        dma((3, 8)),
        dma((3, 8)),
        dma((3, 8)),
        dma((3, 8)),
        dma((4, 3, 8)),
        dma((4, 3, 8)),
        dma((4, 3, 8)),
        dma((4, 3, 8)),
    ]
    far = pl.BlockSpec(memory_space=pltpu.HBM)
    moved = pl.pallas_call(
        functools.partial(body, devices, ranks, channels),
        out_shape=(
            *shapes,
            jax.ShapeDtypeStruct((2 * channels, RANK), F32),
            jax.ShapeDtypeStruct((3, 1, channels), F32),
        ),
        in_specs=[far] * len(operands),
        out_specs=[far] * 6,
        scratch_shapes=scratch,
        compiler_params=pltpu.CompilerParams(
            collective_id=0, has_side_effects=True, vmem_limit_bytes=VMEM
        ),
    )(*operands)
    rkv, xr, kv, xp, down, up, *vectors = pl.pallas_call(
        functools.partial(results, pairs),
        out_shape=(
            *shapes,
            jax.ShapeDtypeStruct(fading_narrowing.shape, F32),
            jax.ShapeDtypeStruct(fading_widening.shape, F32),
            *[jax.ShapeDtypeStruct((1, channels), F32)] * 3,
        ),
        in_specs=[far] * 6,
        out_specs=[far] * 9,
        scratch_shapes=[pltpu.VMEM(a.shape, a.dtype) for a in moved]
        + [dma((6,)), dma((8 + pairs,))],
        compiler_params=pltpu.CompilerParams(vmem_limit_bytes=VMEM),
    )(*moved)
    return rkv, xr, kv, xp, down, up, *[v.reshape(channels) for v in vectors]


def solution(mesh):
    in_specs = (
        P(None, "dp", None, "mp"),
        P("dp", None, "mp"),
        P(None, "dp", None, "mp"),
        P("dp", None, "mp"),
        P("dp", None, "mp"),
        P(),
        P(),
        P("mp", None),
        P(None, "mp"),
        P("mp"),
        P("mp"),
        P("mp"),
    )
    out_specs = (
        P(None, "dp", None, "mp"),
        P("dp", None, "mp"),
        P(None, "dp", None, "mp"),
        P("dp", None, "mp"),
        P("mp", None),
        P(None, "mp"),
        P("mp"),
        P("mp"),
        P("mp"),
    )
    return jax.shard_map(
        per_device, mesh=mesh, in_specs=in_specs, out_specs=out_specs, check_vma=False
    )
```
